32 devices in a mesh: tm: 4 (over z), space: 8 (over y, x, core).
Axes of the slice: x: 2, y: 2, z: 4, core: 2. Of those that a mesh axis runs over, the one named last changes fastest.
Arguments:
- frames: bfloat16 [4, 73, 64, 1024], P('tm', None, None, 'space'), may hold values from -6 to 6
- regrid_mats: bfloat16 [16, 64, 144], replicated, may hold values from -0.75 to 0.75
- pair_source: int32 [1024], P('space'), may hold values from 0 to 127
- pair_matrix: int32 [1024], P('space'), may hold values from 0 to 15
- pair_device: int32 [1024, 1], P('space'), may hold values from 0 to 7; in each aligned block of 128 rows (0 to 127, 128 to 255, ...) at most 24 rows name the same one
- pair_local: int32 [1024], P('space'), may hold values from 0 to 11
- w_first: bfloat16 [3, 3, 73, 256], replicated, may hold values from -0.25 to 0.25
- b_first: float32 [256], replicated, may hold values from -3 to 3
- w_second: bfloat16 [3, 3, 256, 256], replicated, may hold values from -0.125 to 0.125
- b_second: float32 [256], replicated, may hold values from -3 to 3
Outputs:
- features: bfloat16 [4, 96, 64, 256], P('tm', 'space')
The draws below stay inside these ranges and needn't reach their ends.
Inputs may be any that keep to these rules, and one draw needn't show every extreme that they name: `pair_device`: among the 128 rows of one device no device number appears more than 24 times, and in every draw some device's rows name one device exactly 24 times.
All inputs are finite; a program needn't handle non-finite values.
Results may differ from the reference program's by a relative error of at most 0.0064.
Values may be sent and summed in bfloat16 or wider, within the bound.
A program may use at most 64 MiB of HBM per device.

```python
import math
import jax
import jax.numpy as jnp
import numpy as np
from jax import lax

VARS = 73
CH = 256
SIDE = 8
LON = 1024
SB = 64
NMAT = 16
PAIRS_DEV = 128
BLK_DEV = 12
TIMES = 4
LAT = 64
SRC_DEV = 128
BLOCKS = 96
PAD_SIDE = 12
PAD_CELLS = 144
CAP = 24
N_SPACE = 8


def place_ends(drawn, own_key, least, largest):
    index_at = [jax.random.randint(jax.random.fold_in(own_key, axis), (), 0, length) for axis, length in enumerate(drawn.shape)]
    main_axis = drawn.shape.index(max(drawn.shape))
    neighbour = index_at[:main_axis] + [(index_at[main_axis] + 1) % drawn.shape[main_axis]] + index_at[main_axis + 1:]
    return drawn.at[tuple(index_at)].set(least).at[tuple(neighbour)].set(largest)


def levels(key, extent, cuts, least, top_value):
    def one(position, blocks):
        heights = jax.random.uniform(jax.random.fold_in(jax.random.fold_in(key, 6), position), (blocks,), jnp.float32, least / len(cuts), top_value / len(cuts))
        return jnp.repeat(jnp.exp(heights), extent[position] // blocks).reshape((-1,) + (1,) * (len(extent) - position - 1))

    factor_of = one(*cuts[0])
    for cut in cuts[1:]:
        factor_of = factor_of * one(*cut)
    return factor_of


def shared_out(key, own, number, rows, number_of, top, reach, skew):
    order = jax.random.permutation(key, number_of)
    crowded, usual = portions_of(number_of, rows * top, reach, skew, True), portions_of(number_of, rows * top, reach, skew, False)
    places = jnp.arange(number_of)

    def named(tallies, rotation):
        used = int((tallies > 0).sum())
        fixed = max(1, used // 4)
        shifted = fixed + (places - fixed + rotation * (used - fixed)) % max(1, number_of - fixed)
        return jnp.zeros((number_of,), jnp.int32).at[order[jnp.where(places < fixed, places, shifted)]].set(jnp.asarray(tallies, jnp.int32))

    tallies = jnp.where(number % 4 == 0, named(crowded, number // 4), named(usual, number - number // 4 - 1))
    mixed = jax.random.permutation(jax.random.fold_in(own, 3), number_of)
    giver, receiver = mixed[0:number_of // 2 * 2:2], mixed[1:number_of // 2 * 2:2]
    margin = jnp.minimum(tallies[giver] - 1, reach - tallies[receiver]) // 2
    margin = jnp.where((giver == order[0]) | (receiver == order[0]) | (tallies[receiver] == 0), 0, jnp.maximum(margin, 0))
    shifted = jax.random.randint(jax.random.fold_in(own, 4), (number_of // 2,), 0, 1 << 20) % (margin + 1)
    tallies = tallies.at[giver].add(-shifted).at[receiver].add(shifted)
    labels = jnp.searchsorted(jnp.cumsum(tallies), jnp.arange(rows * top), side="right").astype(jnp.int32)
    table = labels.reshape(top, rows).T
    table = table[jax.random.permutation(jax.random.fold_in(own, 1), rows)]
    rotation = jax.random.randint(jax.random.fold_in(own, 2), (rows, 1), 0, top)
    return jnp.take_along_axis(table, (jnp.arange(top)[None, :] + rotation) % top, axis=1)


def portions_of(amount, total, reach, lean, full):
    portions = [(1 << 20) // math.isqrt(standing ** lean) + 1 for standing in range(1, amount + 1)]
    largest = reach if full else min(reach, max(-(-total // amount), total * portions[0] // sum(portions)))
    least = 1 if total - largest >= amount - 1 else 0
    holding, spare = [largest] + [least] * (amount - 1), total - largest - least * (amount - 1)
    while spare > 0:
        movable = [i for i in range(1, amount) if holding[i] < largest] or [i for i in range(1, amount) if holding[i] < reach]
        whole, left = sum([portions[i] for i in movable]), spare
        for i in movable:
            more = min(reach - holding[i], max(1, left * portions[i] // whole), spare)
            holding[i] = holding[i] + more
            spare = spare - more
    return np.array(holding)


def scatter_about(rng, dims, width, most, pieces=(), held_as=jnp.bfloat16):
    factor_of = levels(rng, dims, pieces, -0.22, 0.18) if pieces else 1.0
    result = jax.random.normal(rng, dims, jnp.float32) * width * factor_of
    return jnp.minimum(jnp.maximum(result, -most), most).astype(held_as)


def setup_inputs(seed: int = 0) -> dict:
    keys = jax.random.split(jax.random.key(seed), 11)
    frames = scatter_about(keys[0], (TIMES, VARS, LAT, LON), 1.0, 6.0, ((0, 4), (3, 8)))
    regrid_mats = scatter_about(keys[1], (NMAT, SB, PAD_CELLS), SB ** -0.5, 0.75)
    pair_source = place_ends(jax.random.randint(keys[2], (N_SPACE * PAIRS_DEV,), 0, SRC_DEV), jax.random.fold_in(keys[2], 1), 0, SRC_DEV - 1).astype(jnp.int32)
    pair_matrix = place_ends(jax.random.randint(keys[3], (N_SPACE * PAIRS_DEV,), 0, NMAT), jax.random.fold_in(keys[3], 1), 0, NMAT - 1).astype(jnp.int32)
    pair_device_keys = jax.random.split(jax.random.fold_in(keys[4], 1), (N_SPACE * PAIRS_DEV) // PAIRS_DEV)
    pair_device_turns = jax.random.permutation(jax.random.fold_in(keys[4], 3), (N_SPACE * PAIRS_DEV) // PAIRS_DEV)
    pair_device = jax.vmap(lambda own, number: shared_out(jax.random.fold_in(keys[4], 2), own, number, PAIRS_DEV, N_SPACE, 1, CAP, 2))(pair_device_keys, pair_device_turns).reshape((N_SPACE * PAIRS_DEV, 1))
    pair_local = place_ends(jax.random.randint(keys[5], (N_SPACE * PAIRS_DEV,), 0, BLK_DEV), jax.random.fold_in(keys[5], 1), 0, BLK_DEV - 1).astype(jnp.int32)
    w_first = scatter_about(keys[6], (3, 3, VARS, CH), (9 * VARS) ** -0.5, 0.25)
    b_first = scatter_about(keys[7], (CH,), 0.5, 3.0, (), jnp.float32)
    w_second = scatter_about(keys[8], (3, 3, CH, CH), (9 * CH) ** -0.5, 0.125)
    b_second = scatter_about(keys[9], (CH,), 0.5, 3.0, (), jnp.float32)
    return {"frames": frames, "regrid_mats": regrid_mats, "pair_source": pair_source, "pair_matrix": pair_matrix, "pair_device": pair_device, "pair_local": pair_local, "w_first": w_first, "b_first": b_first, "w_second": w_second, "b_second": b_second}


def conv_valid(inputs, weights, layout):
    return lax.conv_general_dilated(inputs, weights, (1, 1), "VALID", dimension_numbers=layout, precision=lax.Precision.HIGHEST, preferred_element_type=jnp.float32)


def encode(group_field, w_first, b_first, w_second, b_second):
    block_count = group_field.shape[0]
    images = group_field.reshape(block_count * TIMES, VARS, PAD_SIDE, PAD_SIDE).astype(jnp.float32)
    first_out = conv_valid(images, w_first.astype(jnp.float32), ("NCHW", "HWIO", "NHWC")) + b_first
    hidden = jax.nn.gelu(first_out, approximate=True).astype(jnp.bfloat16)
    second = conv_valid(hidden.astype(jnp.float32), w_second.astype(jnp.float32), ("NHWC", "HWIO", "NHWC")) + b_second
    return second.astype(jnp.bfloat16).reshape(block_count, TIMES, SIDE * SIDE, CH)


def reference(frames, regrid_mats, pair_source, pair_matrix, pair_device, pair_local, w_first, b_first, w_second, b_second):
    source = frames.reshape(TIMES, VARS, N_SPACE * SRC_DEV, SB)
    source_rows = pair_source.reshape(N_SPACE, PAIRS_DEV)
    matrix_rows = pair_matrix.reshape(N_SPACE, PAIRS_DEV)
    target_rows = (pair_device[:, 0] * BLK_DEV + pair_local).astype(jnp.int32).reshape(N_SPACE, PAIRS_DEV)

    def add_sender(padded_field, inputs):
        sender, source_ids, matrix_ids, block_ids = inputs
        picked = jnp.take(source, (sender * SRC_DEV + source_ids).astype(jnp.int32), axis=2).astype(jnp.float32)
        matrices = jnp.take(regrid_mats, matrix_ids, axis=0).astype(jnp.float32)
        partial_value = jnp.einsum("tvps,psc->ptvc", picked, matrices, precision=lax.Precision.HIGHEST).astype(jnp.bfloat16)
        return padded_field.at[block_ids].add(partial_value.astype(jnp.float32)), None

    padded_field = jnp.zeros((BLOCKS, TIMES, VARS, PAD_CELLS), jnp.float32)
    senders = jnp.arange(N_SPACE, dtype=jnp.int32)
    padded_field, unused = lax.scan(add_sender, padded_field, (senders, source_rows, matrix_rows, target_rows))
    grouped = padded_field.astype(jnp.bfloat16).reshape(N_SPACE, BLK_DEV, TIMES, VARS, PAD_SIDE, PAD_SIDE)
    encoded = lax.map(lambda group_field: encode(group_field, w_first, b_first, w_second, b_second), grouped)
    return jnp.transpose(encoded.reshape(BLOCKS, TIMES, SIDE * SIDE, CH), (1, 0, 2, 3))
```

```python
import functools

import jax
import jax.numpy as jnp
from jax import lax
from jax.experimental import pallas as pl
from jax.experimental.pallas import tpu as pltpu
from jax.sharding import PartitionSpec as P

SIDE = 8
SB = 64
BLK_DEV = 12
PAD_SIDE = 12

MESH = pl.DeviceIdType.MESH
VMEM = pl.BlockSpec(memory_space=pltpu.VMEM)
LANES = 128
ROW = 16
GROUP = 4
CHUNKS = 3
MATCH = 1 << 20


def greet(peers):
    barrier = pltpu.get_barrier_semaphore()
    for peer in peers:
        pl.semaphore_signal(barrier, inc=1, device_id={"space": peer}, device_id_type=MESH)
    pl.semaphore_wait(barrier, len(peers))


def table_kernel(devices, table_ref, all_ref, send_sem, recv_sem):
    me = lax.axis_index("space")
    greet([lax.rem(me + step, devices) for step in range(1, devices)])
    copies = []
    for step in range(1, devices):
        copy = pltpu.make_async_remote_copy(
            src_ref=table_ref,
            dst_ref=all_ref.at[me],
            send_sem=send_sem.at[step],
            recv_sem=recv_sem.at[step],
            device_id={"space": lax.rem(me + step, devices)},
            device_id_type=MESH,
        )
        copy.start()
        copies.append(copy)
    all_ref[me] = table_ref[...]
    for copy in copies:
        copy.wait()


def gather_tables(table, devices):
    return pl.pallas_call(
        functools.partial(table_kernel, devices),
        out_shape=jax.ShapeDtypeStruct((devices,) + table.shape, table.dtype),
        in_specs=[VMEM],
        out_specs=VMEM,
        scratch_shapes=[
            pltpu.SemaphoreType.DMA((devices,)),
            pltpu.SemaphoreType.DMA((devices,)),
        ],
        compiler_params=pltpu.CompilerParams(collective_id=0, has_side_effects=True),
        name="pair_tables",
    )(table)


def regrid_kernel(
    strip_blocks, row_blocks, table_ref, frames_ref, mats_ref, out_ref,
    wide, total, words_v, words_s, chosen, sem,
):
    devices, _, pairs = table_ref.shape
    variables, lats, lanes = frames_ref.shape
    padded = wide.shape[0] // lats
    blocks = out_ref.shape[0]
    me = lax.axis_index("space")
    source = table_ref[:, 0, :]
    matrix = table_ref[:, 1, :]
    target = table_ref[:, 2, :] * BLK_DEV + table_ref[:, 3, :]
    band = lax.broadcasted_iota(jnp.int32, (devices, pairs), 0)
    lat = band * (lats // devices) + source // row_blocks
    place = source % row_blocks
    mine = (place // strip_blocks) == me
    word = target * 2048 + lat * 32 + matrix * strip_blocks + place % strip_blocks
    words_v[...] = word + jnp.where(mine, MATCH, 0)
    move = pltpu.make_async_copy(words_v, words_s, sem)
    move.start()

    wide[pl.ds(variables * lats, (padded - variables) * lats), :] = jnp.zeros(
        ((padded - variables) * lats, lanes), jnp.float32
    )

    @pl.loop(0, variables)
    def _(v):
        wide[pl.ds(pl.multiple_of(v * lats, lats), lats), :] = frames_ref[v].astype(jnp.float32)

    @pl.loop(0, blocks + 1)
    def _(b):
        total[b] = jnp.zeros(total.shape[1:], jnp.float32)

    move.wait()

    def scan_row(row, count):
        def scan(step, count):
            for lane in range(8):
                value = words_s[row, step * 8 + lane]
                chosen[count] = value
                count = count + (value >> 20)
            return count

        return lax.fori_loop(0, pairs // 8, scan, count)

    count = lax.fori_loop(0, devices, scan_row, 0)
    for extra in range(GROUP):
        chosen[count + extra] = blocks * 2048

    @pl.loop(0, (count + GROUP - 1) // GROUP)
    def _(step):
        products, homes = [], []
        for lane in range(GROUP):
            value = chosen[step * GROUP + lane] & (MATCH - 1)
            homes.append(value >> 11)
            cells = wide[pl.ds((value >> 5) & 63, padded, stride=lats), :].astype(jnp.bfloat16)
            products.append(
                lax.dot_general(
                    mats_ref[value & 31], cells, (((1,), (1,)), ((), ())),
                    preferred_element_type=jnp.float32,
                )
            )
        for home, product in zip(homes, products):
            total[home, :, :padded] += product

    @pl.loop(0, blocks)
    def _(b):
        out_ref[b] = total[b].astype(jnp.bfloat16)


def regrid(tables, frames, mats, blocks, strip_blocks, row_blocks):
    devices, _, pairs = tables.shape
    variables, lats, lanes = frames.shape
    padded = -(-variables // 16) * 16
    cells = mats.shape[1]
    return pl.pallas_call(
        functools.partial(regrid_kernel, strip_blocks, row_blocks),
        out_shape=jax.ShapeDtypeStruct((blocks, cells, LANES), jnp.bfloat16),
        in_specs=[VMEM] * 3,
        out_specs=VMEM,
        scratch_shapes=[
            pltpu.VMEM((padded * lats, lanes), jnp.float32),
            pltpu.VMEM((blocks + 1, cells, LANES), jnp.float32),
            pltpu.VMEM((devices, pairs), jnp.int32),
            pltpu.SMEM((devices, pairs), jnp.int32),
            pltpu.SMEM((devices * pairs + 8,), jnp.int32),
            pltpu.SemaphoreType.DMA,
        ],
        compiler_params=pltpu.CompilerParams(vmem_limit_bytes=40 << 20),
        name="regrid_pairs",
    )(tables, frames, mats)


def encode_kernel(
    chips, part_ref, w1_ref, b1_ref, w2_ref, b2_ref, out_ref,
    near, sums, far, flat, wide, hid, taps,
    near_send, near_recv, far_send, far_recv,
):
    me = lax.axis_index("space")
    chip, core = me // 2, lax.rem(me, 2)
    size = BLK_DEV // CHUNKS
    cells = part_ref.shape[1]
    order = list(range(1, chips)) + [0]
    peers = [lax.rem(chip + step, chips) for step in range(chips)]
    sibling = chip * 2 + 1 - core
    greet([sibling] + [peers[step] * 2 + core for step in range(1, chips)])

    near_copies = {}
    for chunk in range(CHUNKS):
        for step in order:
            first = (peers[step] * 2 + 1 - core) * BLK_DEV + chunk * size
            copy = pltpu.make_async_remote_copy(
                src_ref=part_ref.at[pl.ds(first, size)],
                dst_ref=near.at[step, pl.ds(chunk * size, size)],
                send_sem=near_send.at[chunk, step],
                recv_sem=near_recv.at[chunk, step],
                device_id={"space": sibling},
                device_id_type=MESH,
            )
            copy.start()
            near_copies[chunk, step] = copy

    far_copies = {}
    for chunk in range(CHUNKS):
        for step in order:
            near_copies[chunk, step].wait_recv()
            first = (peers[step] * 2 + core) * BLK_DEV + chunk * size
            here = pl.ds(chunk * size, size)
            sums[step, here] = (
                part_ref[pl.ds(first, size)].astype(jnp.float32)
                + near[step, here].astype(jnp.float32)
            ).astype(jnp.bfloat16)
            if step:
                copy = pltpu.make_async_remote_copy(
                    src_ref=sums.at[step, here],
                    dst_ref=far.at[step - 1, here],
                    send_sem=far_send.at[chunk, step],
                    recv_sem=far_recv.at[chunk, step],
                    device_id={"space": peers[step] * 2 + core},
                    device_id_type=MESH,
                )
                copy.start()
                far_copies[chunk, step] = copy

    side = PAD_SIDE
    mid = side - 2
    last = side - 4
    for chunk in range(CHUNKS):
        here = pl.ds(chunk * size, size)
        for step in range(1, chips):
            far_copies[chunk, step].wait_recv()
        for b in range(size):
            field = sums[0, chunk * size + b].astype(jnp.float32)
            for step in range(1, chips):
                field = field + far[step - 1, chunk * size + b].astype(jnp.float32)
            flat[pl.ds(0, cells), :] = field
            for i in range(side):
                for c in range(3):
                    wide[b, i, :, c * LANES:(c + 1) * LANES] = flat[
                        pl.ds(i * side + c, ROW), :
                    ].astype(jnp.bfloat16)
        first_out = b1_ref[...]
        for a in range(3):
            rows = wide[:, a:a + mid].reshape(size * mid * ROW, 3 * LANES)
            first_out = first_out + jnp.dot(rows, w1_ref[a], preferred_element_type=jnp.float32)
        hid[pl.ds(0, size * mid * ROW), :] = jax.nn.gelu(first_out, approximate=True)
        channels = hid.shape[1]
        for c in range(3):
            taps[:, c * channels:(c + 1) * channels] = hid[
                pl.ds(c, size * mid * ROW), :
            ].astype(jnp.bfloat16)
        shifted = taps[...].reshape(size, mid, ROW, 3 * channels)
        second = b2_ref[...]
        for a in range(3):
            rows = shifted[:, a:a + last].reshape(size * last * ROW, 3 * channels)
            second = second + jnp.dot(rows, w2_ref[a], preferred_element_type=jnp.float32)
        second = second.reshape(size, last, ROW, -1)[:, :, :last, :]
        out_ref[here] = second.reshape(size, last * last, -1).astype(jnp.bfloat16)

    for copy in list(near_copies.values()) + list(far_copies.values()):
        copy.wait_send()


def encode(part, w1, b1, w2, b2, chips):
    cells = part.shape[1]
    channels = w2.shape[-1]
    hidden = w1.shape[-1]
    size = BLK_DEV // CHUNKS
    rows = size * (PAD_SIDE - 2) * ROW
    semaphores = [pltpu.SemaphoreType.DMA((CHUNKS, chips))] * 4
    return pl.pallas_call(
        functools.partial(encode_kernel, chips),
        out_shape=jax.ShapeDtypeStruct((BLK_DEV, SIDE * SIDE, channels), jnp.bfloat16),
        in_specs=[VMEM] * 5,
        out_specs=VMEM,
        scratch_shapes=[
            pltpu.VMEM((chips, BLK_DEV, cells, LANES), jnp.bfloat16),
            pltpu.VMEM((chips, BLK_DEV, cells, LANES), jnp.bfloat16),
            pltpu.VMEM((chips - 1, BLK_DEV, cells, LANES), jnp.bfloat16),
            pltpu.VMEM((cells + ROW, LANES), jnp.float32),
            pltpu.VMEM((size, PAD_SIDE, ROW, 3 * LANES), jnp.bfloat16),
            pltpu.VMEM((rows + ROW, hidden), jnp.float32),
            pltpu.VMEM((rows, 3 * hidden), jnp.bfloat16),
        ] + semaphores,
        compiler_params=pltpu.CompilerParams(
            collective_id=1, has_side_effects=True, vmem_limit_bytes=40 << 20
        ),
        name="reduce_and_encode",
    )(part, w1, b1, w2, b2)


def strips(
    frames,
    regrid_mats,
    pair_source,
    pair_matrix,
    pair_device,
    pair_local,
    w_first,
    b_first,
    w_second,
    b_second,
):
    devices = lax.axis_size("space")
    strip_blocks = frames.shape[3] // SB
    row_blocks = strip_blocks * devices
    table = jnp.stack([pair_source, pair_matrix, pair_device[:, 0], pair_local])
    tables = gather_tables(table, devices)
    turned = jnp.transpose(regrid_mats, (0, 2, 1))
    mats = jnp.stack(
        [
            jnp.pad(turned, ((0, 0), (0, 0), (place * SB, (strip_blocks - 1 - place) * SB)))
            for place in range(strip_blocks)
        ],
        axis=1,
    ).reshape(-1, turned.shape[1], strip_blocks * SB)
    part = regrid(tables, frames[0], mats, devices * BLK_DEV, strip_blocks, row_blocks)
    lift = LANES - w_first.shape[2]
    w1 = jnp.pad(w_first, ((0, 0), (0, 0), (0, lift), (0, 0))).reshape(3, 3 * LANES, -1)
    w2 = w_second.reshape(3, -1, w_second.shape[-1])
    out = encode(part, w1, b_first[None], w2, b_second[None], devices // 2)
    return out[None]


def conv_valid(inputs, weights, layout):
    return lax.conv_general_dilated(
        inputs,
        weights,
        (1, 1),
        "VALID",
        dimension_numbers=layout,
        preferred_element_type=jnp.float32,
    )


def per_device(
    frames,
    regrid_mats,
    pair_source,
    pair_matrix,
    pair_device,
    pair_local,
    w_first,
    b_first,
    w_second,
    b_second,
):
    devices = lax.axis_size("space")
    band_rows = lax.all_to_all(frames, "space", split_axis=2, concat_axis=3, tiled=True)
    local_times = band_rows.shape[0]
    variables = band_rows.shape[1]
    source = band_rows.reshape(local_times, variables, -1, SB)
    pair_count = pair_source.shape[0]
    capacity = max(2, 3 * pair_count // (2 * devices))
    flat_count = devices * capacity
    target = pair_device[:, 0]
    matches = (target[:, None] == jnp.arange(devices, dtype=jnp.int32)[None, :]).astype(jnp.int32)
    ranking = jnp.sum(matches * (jnp.cumsum(matches, axis=0) - 1), axis=1)
    places = target * capacity + ranking
    block_slots = (
        jnp.full((flat_count,), BLK_DEV, jnp.int32)
        .at[places]
        .set(pair_local)
        .reshape(devices, capacity)
    )
    picked = jnp.take(source, pair_source, axis=2)
    shipped = jnp.transpose(picked, (2, 0, 1, 3))
    outgoing = (
        jnp.zeros((flat_count, local_times, variables, SB), jnp.bfloat16).at[places].set(shipped)
    )
    outgoing = outgoing.reshape(devices, capacity, local_times, variables, SB)
    matrix_slots = (
        jnp.zeros((flat_count,), jnp.int32).at[places].set(pair_matrix).reshape(devices, capacity)
    )
    rows_part = lax.all_to_all(outgoing, "space", split_axis=0, concat_axis=0, tiled=True)
    matrix_part = lax.all_to_all(matrix_slots, "space", split_axis=0, concat_axis=0, tiled=True)
    block_part = lax.all_to_all(block_slots, "space", split_axis=0, concat_axis=0, tiled=True)
    matrices = jnp.take(regrid_mats, matrix_part, axis=0)
    partial_value = jnp.einsum(
        "nktvs,nksc->nktvc", rows_part, matrices, preferred_element_type=jnp.float32
    ).astype(jnp.bfloat16)
    selector = (
        block_part.reshape(1, flat_count) == jnp.arange(BLK_DEV, dtype=jnp.int32)[:, None]
    ).astype(jnp.bfloat16)
    summed = jnp.dot(
        selector, partial_value.reshape(flat_count, -1), preferred_element_type=jnp.float32
    )
    padded_field = summed.astype(jnp.bfloat16).reshape(
        BLK_DEV * local_times, variables, PAD_SIDE, PAD_SIDE
    )
    first_out = conv_valid(padded_field, w_first, ("NCHW", "HWIO", "NHWC")) + b_first
    hidden = jax.nn.gelu(first_out, approximate=True).astype(jnp.bfloat16)
    second = conv_valid(hidden, w_second, ("NHWC", "HWIO", "NHWC")) + b_second
    result = second.astype(jnp.bfloat16).reshape(BLK_DEV, local_times, SIDE * SIDE, -1)
    return jnp.transpose(result, (1, 0, 2, 3))


def solution(mesh):
    in_specs = (
        P("tm", None, None, "space"),
        P(),
        P("space"),
        P("space"),
        P("space", None),
        P("space"),
        P(),
        P(),
        P(),
        P(),
    )
    out_specs = P("tm", "space", None, None)
    devices = mesh.shape["space"]

    def program(frames, *rest):
        local = (frames.shape[0] // mesh.shape["tm"], frames.shape[3] // devices)
        whole_blocks = local == (1, LANES) and LANES % SB == 0 and devices % 2 == 0
        body = strips if whole_blocks and frames.shape[2] <= SB else per_device
        return jax.shard_map(
            body, mesh=mesh, in_specs=in_specs, out_specs=out_specs, check_vma=False
        )(frames, *rest)

    return program
```

```python
import functools

import jax
import jax.numpy as jnp
from jax import lax
from jax.experimental import pallas as pl
from jax.experimental.pallas import tpu as pltpu
from jax.sharding import PartitionSpec as P

SIDE = 8
SB = 64
BLK_DEV = 12
PAD_SIDE = 12

MESH = pl.DeviceIdType.MESH
VMEM = pl.BlockSpec(memory_space=pltpu.VMEM)
LANES = 128
ROW = 16
GROUP = 4
CHUNKS = 3
MATCH = 1 << 20
FRONT = 64
TAIL = 16


def greet(peers):
    barrier = pltpu.get_barrier_semaphore()
    for peer in peers:
        pl.semaphore_signal(barrier, inc=1, device_id={"space": peer}, device_id_type=MESH)
    pl.semaphore_wait(barrier, len(peers))


def table_kernel(devices, table_ref, mats_ref, all_ref, turned_ref, send_sem, recv_sem):
    me = lax.axis_index("space")
    greet([lax.rem(me + step, devices) for step in range(1, devices)])
    copies = []
    for step in range(1, devices):
        copy = pltpu.make_async_remote_copy(
            src_ref=table_ref,
            dst_ref=all_ref.at[me],
            send_sem=send_sem.at[step],
            recv_sem=recv_sem.at[step],
            device_id={"space": lax.rem(me + step, devices)},
            device_id_type=MESH,
        )
        copy.start()
        copies.append(copy)
    all_ref[me] = table_ref[...]
    strip_blocks = turned_ref.shape[0] // mats_ref.shape[0]

    @pl.loop(0, mats_ref.shape[0])
    def _(m):
        matrix = mats_ref[m].astype(jnp.float32)
        blank = jnp.zeros_like(matrix)
        for place in range(strip_blocks):
            stack = [matrix if other == place else blank for other in range(strip_blocks)]
            turned_ref[m * strip_blocks + place] = (
                jnp.concatenate(stack, axis=0).T.astype(jnp.bfloat16)
            )

    for copy in copies:
        copy.wait()


def gather_tables(table, mats, devices, strip_blocks):
    turned = (mats.shape[0] * strip_blocks, mats.shape[2], strip_blocks * mats.shape[1])
    return pl.pallas_call(
        functools.partial(table_kernel, devices),
        out_shape=(
            jax.ShapeDtypeStruct((devices,) + table.shape, table.dtype),
            jax.ShapeDtypeStruct(turned, mats.dtype),
        ),
        in_specs=[VMEM] * 2,
        out_specs=(VMEM, VMEM),
        scratch_shapes=[
            pltpu.SemaphoreType.DMA((devices,)),
            pltpu.SemaphoreType.DMA((devices,)),
        ],
        compiler_params=pltpu.CompilerParams(collective_id=0, has_side_effects=True, vmem_limit_bytes=16 << 20),
        name="pair_tables",
    )(table, mats)


def regrid_kernel(
    strip_blocks, row_blocks, table_ref, frames_ref, mats_ref, out_ref,
    wide, total, words_v, words_s, chosen, sem,
):
    devices, _, pairs = table_ref.shape
    variables, lats, lanes = frames_ref.shape
    padded = wide.shape[0] // lats
    blocks = out_ref.shape[0]
    me = lax.axis_index("space")
    source = table_ref[:, 0, :]
    matrix = table_ref[:, 1, :]
    target = table_ref[:, 2, :] * BLK_DEV + table_ref[:, 3, :]
    band = lax.broadcasted_iota(jnp.int32, (devices, pairs), 0)
    lat = band * (lats // devices) + source // row_blocks
    place = source % row_blocks
    mine = (place // strip_blocks) == me
    word = target * 2048 + lat * 32 + matrix * strip_blocks + place % strip_blocks
    words_v[...] = word + jnp.where(mine, MATCH, 0)
    move = pltpu.make_async_copy(words_v, words_s, sem)
    move.start()

    wide[pl.ds(variables * lats, (padded - variables) * lats), :] = jnp.zeros(
        ((padded - variables) * lats, lanes), jnp.float32
    )

    @pl.loop(0, variables)
    def _(v):
        wide[pl.ds(pl.multiple_of(v * lats, lats), lats), :] = frames_ref[v].astype(jnp.float32)

    @pl.loop(0, blocks + 1)
    def _(b):
        total[b] = jnp.zeros(total.shape[1:], jnp.float32)

    move.wait()

    def scan_row(row, count):
        def scan(step, count):
            values = [words_s[row, step * 16 + lane] for lane in range(16)]
            places = [count]
            for value in values:
                places.append(places[-1] + (value >> 20))
            for value, place in zip(values, places):
                chosen[place] = value
            return places[-1]

        return lax.fori_loop(0, pairs // 16, scan, count)

    count = lax.fori_loop(0, devices, scan_row, 0)
    for extra in range(GROUP):
        chosen[count + extra] = blocks * 2048

    @pl.loop(0, (count + GROUP - 1) // GROUP)
    def _(step):
        products, homes = [], []
        for lane in range(GROUP):
            value = chosen[step * GROUP + lane] & (MATCH - 1)
            homes.append(value >> 11)
            cells = wide[pl.ds((value >> 5) & 63, padded, stride=lats), :].astype(jnp.bfloat16)
            products.append(
                lax.dot_general(
                    mats_ref[value & 31], cells, (((1,), (1,)), ((), ())),
                    preferred_element_type=jnp.float32,
                )
            )
        for home, product in zip(homes, products):
            total[home, :, :padded] += product

    @pl.loop(0, blocks)
    def _(b):
        out_ref[b] = total[b].astype(jnp.bfloat16)


def regrid(tables, frames, mats, blocks, strip_blocks, row_blocks):
    devices, _, pairs = tables.shape
    variables, lats, lanes = frames.shape
    padded = -(-variables // 16) * 16
    cells = mats.shape[1]
    return pl.pallas_call(
        functools.partial(regrid_kernel, strip_blocks, row_blocks),
        out_shape=jax.ShapeDtypeStruct((blocks, cells, LANES), jnp.bfloat16),
        in_specs=[VMEM] * 3,
        out_specs=VMEM,
        scratch_shapes=[
            pltpu.VMEM((padded * lats, lanes), jnp.float32),
            pltpu.VMEM((blocks + 1, cells, LANES), jnp.float32),
            pltpu.VMEM((devices, pairs), jnp.int32),
            pltpu.SMEM((devices, pairs), jnp.int32),
            pltpu.SMEM((devices * pairs + 8,), jnp.int32),
            pltpu.SemaphoreType.DMA,
        ],
        compiler_params=pltpu.CompilerParams(vmem_limit_bytes=40 << 20),
        name="regrid_pairs",
    )(tables, frames, mats)


def pack_fields(fields):
    half = fields[0].shape[0] // 2
    lane = lax.broadcasted_iota(jnp.int32, (half, LANES), 1)
    rest = jnp.zeros((half, LANES), jnp.float32)
    rows = []
    for b, field in enumerate(fields):
        upper, lower = field[:half], field[half:]
        rows.append(jnp.where(lane < FRONT, upper, pltpu.roll(lower, FRONT, 1)))
        for side, piece in enumerate((upper, lower)):
            start = (2 * b + side) * TAIL
            moved = pltpu.roll(piece, (start - FRONT) % LANES, 1)
            rest = jnp.where((lane >= start) & (lane < start + TAIL), moved, rest)
    rows.append(rest)
    spare = -len(rows) * half % ROW
    if spare:
        rows.append(jnp.zeros((spare, LANES), jnp.float32))
    return jnp.concatenate(rows, axis=0)


def unpack_field(packed, b, size, cells):
    half = cells // 2
    lane = lax.broadcasted_iota(jnp.int32, (half, LANES), 1)
    front = packed[b * half:(b + 1) * half]
    rest = packed[size * half:(size + 1) * half]
    pieces = []
    for side in range(2):
        start = (2 * b + side) * TAIL
        head = pltpu.roll(front, FRONT, 1) if side else front
        tail = pltpu.roll(rest, (FRONT - start) % LANES, 1)
        tail = jnp.where(lane < FRONT + TAIL, tail, 0.0)
        pieces.append(jnp.where(lane < FRONT, head, tail))
    return jnp.concatenate(pieces, axis=0)


def encode_kernel(
    chips, part_ref, w1_ref, b1_ref, w2_ref, b2_ref, out_ref,
    near, own, sums, far, flat, wide, hid, taps,
    near_send, near_recv, far_send, far_recv,
):
    me = lax.axis_index("space")
    chip, core = me // 2, lax.rem(me, 2)
    size = BLK_DEV // CHUNKS
    cells = part_ref.shape[1]
    order = list(range(1, chips)) + [0]
    peers = [lax.rem(chip + step, chips) for step in range(chips)]
    sibling = chip * 2 + 1 - core
    greet([sibling] + [peers[step] * 2 + core for step in range(1, chips)])

    near_copies = {}
    for chunk in range(CHUNKS):
        for step in order:
            first = (peers[step] * 2 + 1 - core) * BLK_DEV + chunk * size
            copy = pltpu.make_async_remote_copy(
                src_ref=part_ref.at[pl.ds(first, size)],
                dst_ref=near.at[step, pl.ds(chunk * size, size)],
                send_sem=near_send.at[chunk, step],
                recv_sem=near_recv.at[chunk, step],
                device_id={"space": sibling},
                device_id_type=MESH,
            )
            copy.start()
            near_copies[chunk, step] = copy

    far_copies = {}
    for chunk in range(CHUNKS):
        for step in order:
            near_copies[chunk, step].wait_recv()
            first = (peers[step] * 2 + core) * BLK_DEV + chunk * size
            here = pl.ds(chunk * size, size)
            fields = [
                part_ref[first + b].astype(jnp.float32)
                + near[step, chunk * size + b].astype(jnp.float32)
                for b in range(size)
            ]
            if step == 0:
                for b in range(size):
                    own[chunk * size + b] = fields[b]
            else:
                sums[step - 1, chunk] = pack_fields(fields).astype(jnp.bfloat16)
                copy = pltpu.make_async_remote_copy(
                    src_ref=sums.at[step - 1, chunk],
                    dst_ref=far.at[step - 1, chunk],
                    send_sem=far_send.at[chunk, step],
                    recv_sem=far_recv.at[chunk, step],
                    device_id={"space": peers[step] * 2 + core},
                    device_id_type=MESH,
                )
                copy.start()
                far_copies[chunk, step] = copy

    side = PAD_SIDE
    mid = side - 2
    last = side - 4
    for chunk in range(CHUNKS):
        here = pl.ds(chunk * size, size)
        for step in range(1, chips):
            far_copies[chunk, step].wait_recv()
        packed = far[0, chunk].astype(jnp.float32)
        for step in range(1, chips - 1):
            packed = packed + far[step, chunk].astype(jnp.float32)
        for b in range(size):
            flat[pl.ds(0, cells), :] = own[chunk * size + b] + unpack_field(packed, b, size, cells)
            for i in range(side):
                for c in range(3):
                    wide[b, i, :, c * LANES:(c + 1) * LANES] = flat[
                        pl.ds(i * side + c, ROW), :
                    ].astype(jnp.bfloat16)
        first_out = b1_ref[...]
        for a in range(3):
            rows = wide[:, a:a + mid].reshape(size * mid * ROW, 3 * LANES)
            first_out = first_out + jnp.dot(rows, w1_ref[a], preferred_element_type=jnp.float32)
        hid[pl.ds(0, size * mid * ROW), :] = jax.nn.gelu(first_out, approximate=True)
        channels = hid.shape[1]
        for c in range(3):
            taps[:, c * channels:(c + 1) * channels] = hid[
                pl.ds(c, size * mid * ROW), :
            ].astype(jnp.bfloat16)
        shifted = taps[...].reshape(size, mid, ROW, 3 * channels)
        second = b2_ref[...]
        for a in range(3):
            rows = shifted[:, a:a + last].reshape(size * last * ROW, 3 * channels)
            second = second + jnp.dot(rows, w2_ref[a], preferred_element_type=jnp.float32)
        second = second.reshape(size, last, ROW, -1)[:, :, :last, :]
        out_ref[here] = second.reshape(size, last * last, -1).astype(jnp.bfloat16)

    for copy in list(near_copies.values()) + list(far_copies.values()):
        copy.wait_send()


def encode(part, w1, b1, w2, b2, chips):
    cells = part.shape[1]
    channels = w2.shape[-1]
    hidden = w1.shape[-1]
    size = BLK_DEV // CHUNKS
    rows = size * (PAD_SIDE - 2) * ROW
    packed = -(-(size + 1) * (cells // 2) // ROW) * ROW
    semaphores = [pltpu.SemaphoreType.DMA((CHUNKS, chips))] * 4
    return pl.pallas_call(
        functools.partial(encode_kernel, chips),
        out_shape=jax.ShapeDtypeStruct((BLK_DEV, SIDE * SIDE, channels), jnp.bfloat16),
        in_specs=[VMEM] * 5,
        out_specs=VMEM,
        scratch_shapes=[
            pltpu.VMEM((chips, BLK_DEV, cells, LANES), jnp.bfloat16),
            pltpu.VMEM((BLK_DEV, cells, LANES), jnp.float32),
            pltpu.VMEM((chips - 1, CHUNKS, packed, LANES), jnp.bfloat16),
            pltpu.VMEM((chips - 1, CHUNKS, packed, LANES), jnp.bfloat16),
            pltpu.VMEM((cells + ROW, LANES), jnp.float32),
            pltpu.VMEM((size, PAD_SIDE, ROW, 3 * LANES), jnp.bfloat16),
            pltpu.VMEM((rows + ROW, hidden), jnp.float32),
            pltpu.VMEM((rows, 3 * hidden), jnp.bfloat16),
        ] + semaphores,
        compiler_params=pltpu.CompilerParams(
            collective_id=1, has_side_effects=True, vmem_limit_bytes=40 << 20
        ),
        name="reduce_and_encode",
    )(part, w1, b1, w2, b2)


def strips(
    frames,
    regrid_mats,
    pair_source,
    pair_matrix,
    pair_device,
    pair_local,
    w_first,
    b_first,
    w_second,
    b_second,
):
    devices = lax.axis_size("space")
    strip_blocks = frames.shape[3] // SB
    row_blocks = strip_blocks * devices
    table = jnp.stack([pair_source, pair_matrix, pair_device[:, 0], pair_local])
    tables, mats = gather_tables(table, regrid_mats, devices, strip_blocks)
    part = regrid(tables, frames[0], mats, devices * BLK_DEV, strip_blocks, row_blocks)
    lift = LANES - w_first.shape[2]
    w1 = jnp.pad(w_first, ((0, 0), (0, 0), (0, lift), (0, 0))).reshape(3, 3 * LANES, -1)
    w2 = w_second.reshape(3, -1, w_second.shape[-1])
    out = encode(part, w1, b_first[None], w2, b_second[None], devices // 2)
    return out[None]


def conv_valid(inputs, weights, layout):
    return lax.conv_general_dilated(
        inputs,
        weights,
        (1, 1),
        "VALID",
        dimension_numbers=layout,
        preferred_element_type=jnp.float32,
    )


def per_device(
    frames,
    regrid_mats,
    pair_source,
    pair_matrix,
    pair_device,
    pair_local,
    w_first,
    b_first,
    w_second,
    b_second,
):
    devices = lax.axis_size("space")
    band_rows = lax.all_to_all(frames, "space", split_axis=2, concat_axis=3, tiled=True)
    local_times = band_rows.shape[0]
    variables = band_rows.shape[1]
    source = band_rows.reshape(local_times, variables, -1, SB)
    pair_count = pair_source.shape[0]
    capacity = max(2, 3 * pair_count // (2 * devices))
    flat_count = devices * capacity
    target = pair_device[:, 0]
    matches = (target[:, None] == jnp.arange(devices, dtype=jnp.int32)[None, :]).astype(jnp.int32)
    ranking = jnp.sum(matches * (jnp.cumsum(matches, axis=0) - 1), axis=1)
    places = target * capacity + ranking
    block_slots = (
        jnp.full((flat_count,), BLK_DEV, jnp.int32)
        .at[places]
        .set(pair_local)
        .reshape(devices, capacity)
    )
    picked = jnp.take(source, pair_source, axis=2)
    shipped = jnp.transpose(picked, (2, 0, 1, 3))
    outgoing = (
        jnp.zeros((flat_count, local_times, variables, SB), jnp.bfloat16).at[places].set(shipped)
    )
    outgoing = outgoing.reshape(devices, capacity, local_times, variables, SB)
    matrix_slots = (
        jnp.zeros((flat_count,), jnp.int32).at[places].set(pair_matrix).reshape(devices, capacity)
    )
    rows_part = lax.all_to_all(outgoing, "space", split_axis=0, concat_axis=0, tiled=True)
    matrix_part = lax.all_to_all(matrix_slots, "space", split_axis=0, concat_axis=0, tiled=True)
    block_part = lax.all_to_all(block_slots, "space", split_axis=0, concat_axis=0, tiled=True)
    matrices = jnp.take(regrid_mats, matrix_part, axis=0)
    partial_value = jnp.einsum(
        "nktvs,nksc->nktvc", rows_part, matrices, preferred_element_type=jnp.float32
    ).astype(jnp.bfloat16)
    selector = (
        block_part.reshape(1, flat_count) == jnp.arange(BLK_DEV, dtype=jnp.int32)[:, None]
    ).astype(jnp.bfloat16)
    summed = jnp.dot(
        selector, partial_value.reshape(flat_count, -1), preferred_element_type=jnp.float32
    )
    padded_field = summed.astype(jnp.bfloat16).reshape(
        BLK_DEV * local_times, variables, PAD_SIDE, PAD_SIDE
    )
    first_out = conv_valid(padded_field, w_first, ("NCHW", "HWIO", "NHWC")) + b_first
    hidden = jax.nn.gelu(first_out, approximate=True).astype(jnp.bfloat16)
    second = conv_valid(hidden, w_second, ("NHWC", "HWIO", "NHWC")) + b_second
    result = second.astype(jnp.bfloat16).reshape(BLK_DEV, local_times, SIDE * SIDE, -1)
    return jnp.transpose(result, (1, 0, 2, 3))


def solution(mesh):
    in_specs = (
        P("tm", None, None, "space"),
        P(),
        P("space"),
        P("space"),
        P("space", None),
        P("space"),
        P(),
        P(),
        P(),
        P(),
    )
    out_specs = P("tm", "space", None, None)
    devices = mesh.shape["space"]

    def program(frames, *rest):
        local = (frames.shape[0] // mesh.shape["tm"], frames.shape[3] // devices)
        whole_blocks = local == (1, LANES) and LANES % SB == 0 and devices % 2 == 0
        fits = frames.shape[2] <= 64 and FRONT < frames.shape[1] <= FRONT + TAIL
        body = strips if whole_blocks and fits else per_device
        return jax.shard_map(
            body, mesh=mesh, in_specs=in_specs, out_specs=out_specs, check_vma=False
        )(frames, *rest)

    return program
```

```python
import functools

import jax
import jax.numpy as jnp
from jax import lax
from jax.experimental import pallas as pl
from jax.experimental.pallas import tpu as pltpu
from jax.sharding import PartitionSpec as P

SIDE = 8
SB = 64
BLK_DEV = 12
PAD_SIDE = 12

MESH = pl.DeviceIdType.MESH
VMEM = pl.BlockSpec(memory_space=pltpu.VMEM)
LANES = 128
ROW = 16
GROUP = 8
CHUNKS = 3
MATCH = 1 << 20
FRONT = 64
TAIL = 16


def greet(peers):
    barrier = pltpu.get_barrier_semaphore()
    for peer in peers:
        pl.semaphore_signal(barrier, inc=1, device_id={"space": peer}, device_id_type=MESH)
    pl.semaphore_wait(barrier, len(peers))


def table_kernel(
    devices, table_ref, mats_ref, frames_ref, all_ref, turned_ref, cells_ref, wide, send_sem, recv_sem
):
    me = lax.axis_index("space")
    barrier = pltpu.get_barrier_semaphore()
    for step in range(1, devices):
        peer = lax.rem(me + step, devices)
        pl.semaphore_signal(barrier, inc=1, device_id={"space": peer}, device_id_type=MESH)
    variables, lats, lanes = frames_ref.shape
    padded = cells_ref.shape[1]
    wide[pl.ds(variables * lats, (padded - variables) * lats), :] = jnp.zeros(
        ((padded - variables) * lats, lanes), jnp.float32
    )

    @pl.loop(0, variables)
    def _(v):
        wide[pl.ds(pl.multiple_of(v * lats, lats), lats), :] = frames_ref[v].astype(jnp.float32)

    pl.semaphore_wait(barrier, devices - 1)
    copies = []
    for step in range(1, devices):
        copy = pltpu.make_async_remote_copy(
            src_ref=table_ref,
            dst_ref=all_ref.at[me],
            send_sem=send_sem.at[step],
            recv_sem=recv_sem.at[step],
            device_id={"space": lax.rem(me + step, devices)},
            device_id_type=MESH,
        )
        copy.start()
        copies.append(copy)
    all_ref[me] = table_ref[...]
    strip_blocks = turned_ref.shape[0] // mats_ref.shape[0]

    @pl.loop(0, mats_ref.shape[0])
    def _(m):
        matrix = mats_ref[m].astype(jnp.float32)
        blank = jnp.zeros_like(matrix)
        for place in range(strip_blocks):
            stack = [matrix if other == place else blank for other in range(strip_blocks)]
            turned_ref[m * strip_blocks + place] = (
                jnp.concatenate(stack, axis=0).T.astype(jnp.bfloat16)
            )

    @pl.loop(0, lats)
    def _(lat):
        cells_ref[lat] = wide[pl.ds(lat, padded, stride=lats), :].astype(jnp.bfloat16)

    for copy in copies:
        copy.wait()


def gather_tables(table, mats, frames, devices, strip_blocks):
    variables, lats, lanes = frames.shape
    padded = -(-variables // 16) * 16
    turned = (mats.shape[0] * strip_blocks, mats.shape[2], strip_blocks * mats.shape[1])
    return pl.pallas_call(
        functools.partial(table_kernel, devices),
        out_shape=(
            jax.ShapeDtypeStruct((devices,) + table.shape, table.dtype),
            jax.ShapeDtypeStruct(turned, mats.dtype),
            jax.ShapeDtypeStruct((lats, padded, lanes), frames.dtype),
        ),
        in_specs=[VMEM] * 3,
        out_specs=(VMEM, VMEM, VMEM),
        scratch_shapes=[
            pltpu.VMEM((padded * lats, lanes), jnp.float32),
            pltpu.SemaphoreType.DMA((devices,)),
            pltpu.SemaphoreType.DMA((devices,)),
        ],
        compiler_params=pltpu.CompilerParams(collective_id=0, has_side_effects=True, vmem_limit_bytes=24 << 20),
        name="pair_tables",
    )(table, mats, frames)


def regrid_kernel(
    strip_blocks, row_blocks, table_ref, cells_ref, mats_ref, out_ref,
    total, words_v, words_s, chosen, sem,
):
    devices, _, pairs = table_ref.shape
    lats, padded, _ = cells_ref.shape
    blocks = out_ref.shape[0]
    me = lax.axis_index("space")
    source = table_ref[:, 0, :]
    matrix = table_ref[:, 1, :]
    target = table_ref[:, 2, :] * BLK_DEV + table_ref[:, 3, :]
    band = lax.broadcasted_iota(jnp.int32, (devices, pairs), 0)
    lat = band * (lats // devices) + source // row_blocks
    place = source % row_blocks
    mine = (place // strip_blocks) == me
    word = target * 2048 + lat * 32 + matrix * strip_blocks + place % strip_blocks
    words_v[...] = word + jnp.where(mine, MATCH, 0)
    move = pltpu.make_async_copy(words_v, words_s, sem)
    move.start()
    move.wait()

    def scan_row(row, count):
        def scan(step, count):
            clear = total.shape[0] // (devices * (pairs // 16))
            first = (row * (pairs // 16) + step) * clear
            for b in range(clear):
                total[first + b] = jnp.zeros(total.shape[1:], jnp.float32)
            values = [words_s[row, step * 16 + lane] for lane in range(16)]
            places = [count]
            for value in values:
                places.append(places[-1] + (value >> 20))
            for value, place in zip(values, places):
                chosen[place] = value
            return places[-1]

        return lax.fori_loop(0, pairs // 16, scan, count)

    count = lax.fori_loop(0, devices, scan_row, 0)
    for extra in range(GROUP):
        chosen[count + extra] = blocks * 2048

    @pl.loop(0, (count + GROUP - 1) // GROUP)
    def _(step):
        products, homes = [], []
        for lane in range(GROUP):
            value = chosen[step * GROUP + lane] & (MATCH - 1)
            homes.append(value >> 11)
            products.append(
                lax.dot_general(
                    mats_ref[value & 31], cells_ref[(value >> 5) & 63], (((1,), (1,)), ((), ())),
                    preferred_element_type=jnp.float32,
                )
            )
        for home, product in zip(homes, products):
            total[home, :, :padded] += product

    @pl.loop(0, blocks, unroll=4)
    def _(b):
        out_ref[b] = total[b].astype(jnp.bfloat16)


def regrid(tables, sources, mats, blocks, strip_blocks, row_blocks):
    devices, _, pairs = tables.shape
    cells = mats.shape[1]
    steps = devices * (pairs // 16)
    held = -(-(blocks + 1) // steps) * steps
    return pl.pallas_call(
        functools.partial(regrid_kernel, strip_blocks, row_blocks),
        out_shape=jax.ShapeDtypeStruct((blocks, cells, LANES), jnp.bfloat16),
        in_specs=[VMEM] * 3,
        out_specs=VMEM,
        scratch_shapes=[
            pltpu.VMEM((held, cells, LANES), jnp.float32),
            pltpu.VMEM((devices, pairs), jnp.int32),
            pltpu.SMEM((devices, pairs), jnp.int32),
            pltpu.SMEM((devices * pairs + GROUP,), jnp.int32),
            pltpu.SemaphoreType.DMA,
        ],
        compiler_params=pltpu.CompilerParams(vmem_limit_bytes=40 << 20),
        name="regrid_pairs",
    )(tables, sources, mats)


def pack_fields(fields):
    half = fields[0].shape[0] // 2
    lane = lax.broadcasted_iota(jnp.int32, (half, LANES), 1)
    rest = jnp.zeros((half, LANES), jnp.float32)
    rows = []
    for b, field in enumerate(fields):
        upper, lower = field[:half], field[half:]
        rows.append(jnp.where(lane < FRONT, upper, pltpu.roll(lower, FRONT, 1)))
        for side, piece in enumerate((upper, lower)):
            start = (2 * b + side) * TAIL
            moved = pltpu.roll(piece, (start - FRONT) % LANES, 1)
            rest = jnp.where((lane >= start) & (lane < start + TAIL), moved, rest)
    rows.append(rest)
    spare = -len(rows) * half % ROW
    if spare:
        rows.append(jnp.zeros((spare, LANES), jnp.float32))
    return jnp.concatenate(rows, axis=0)


def unpack_field(packed, b, size, cells):
    half = cells // 2
    lane = lax.broadcasted_iota(jnp.int32, (half, LANES), 1)
    front = packed[b * half:(b + 1) * half]
    rest = packed[size * half:(size + 1) * half]
    pieces = []
    for side in range(2):
        start = (2 * b + side) * TAIL
        head = pltpu.roll(front, FRONT, 1) if side else front
        tail = pltpu.roll(rest, (FRONT - start) % LANES, 1)
        tail = jnp.where(lane < FRONT + TAIL, tail, 0.0)
        pieces.append(jnp.where(lane < FRONT, head, tail))
    return jnp.concatenate(pieces, axis=0)


def encode_kernel(
    chips, part_ref, w1_ref, b1_ref, w2_ref, b2_ref, out_ref,
    near, own, sums, far, flat, wide, hid, taps,
    near_send, near_recv, far_send, far_recv,
):
    me = lax.axis_index("space")
    chip, core = me // 2, lax.rem(me, 2)
    size = BLK_DEV // CHUNKS
    cells = part_ref.shape[1]
    order = list(range(1, chips)) + [0]
    peers = [lax.rem(chip + step, chips) for step in range(chips)]
    sibling = chip * 2 + 1 - core
    greet([sibling] + [peers[step] * 2 + core for step in range(1, chips)])

    near_copies = {}
    for chunk in range(CHUNKS):
        for step in order:
            first = (peers[step] * 2 + 1 - core) * BLK_DEV + chunk * size
            copy = pltpu.make_async_remote_copy(
                src_ref=part_ref.at[pl.ds(first, size)],
                dst_ref=near.at[step, pl.ds(chunk * size, size)],
                send_sem=near_send.at[chunk, step],
                recv_sem=near_recv.at[chunk, step],
                device_id={"space": sibling},
                device_id_type=MESH,
            )
            copy.start()
            near_copies[chunk, step] = copy

    far_copies = {}
    for chunk in range(CHUNKS):
        for step in order:
            near_copies[chunk, step].wait_recv()
            first = (peers[step] * 2 + core) * BLK_DEV + chunk * size
            here = pl.ds(chunk * size, size)
            fields = [
                part_ref[first + b].astype(jnp.float32)
                + near[step, chunk * size + b].astype(jnp.float32)
                for b in range(size)
            ]
            if step == 0:
                for b in range(size):
                    own[chunk * size + b] = fields[b]
            else:
                sums[step - 1, chunk] = pack_fields(fields).astype(jnp.bfloat16)
                copy = pltpu.make_async_remote_copy(
                    src_ref=sums.at[step - 1, chunk],
                    dst_ref=far.at[step - 1, chunk],
                    send_sem=far_send.at[chunk, step],
                    recv_sem=far_recv.at[chunk, step],
                    device_id={"space": peers[step] * 2 + core},
                    device_id_type=MESH,
                )
                copy.start()
                far_copies[chunk, step] = copy

    side = PAD_SIDE
    mid = side - 2
    last = side - 4
    for chunk in range(CHUNKS):
        here = pl.ds(chunk * size, size)
        for step in range(1, chips):
            far_copies[chunk, step].wait_recv()
        packed = far[0, chunk].astype(jnp.float32)
        for step in range(1, chips - 1):
            packed = packed + far[step, chunk].astype(jnp.float32)
        for b in range(size):
            flat[pl.ds(0, cells), :] = own[chunk * size + b] + unpack_field(packed, b, size, cells)
            for i in range(side):
                for c in range(3):
                    wide[b, i, :, c * LANES:(c + 1) * LANES] = flat[
                        pl.ds(i * side + c, ROW), :
                    ].astype(jnp.bfloat16)
        first_out = b1_ref[...]
        for a in range(3):
            rows = wide[:, a:a + mid].reshape(size * mid * ROW, 3 * LANES)
            first_out = first_out + jnp.dot(rows, w1_ref[a], preferred_element_type=jnp.float32)
        hid[pl.ds(0, size * mid * ROW), :] = jax.nn.gelu(first_out, approximate=True)
        channels = hid.shape[1]
        for c in range(3):
            taps[:, c * channels:(c + 1) * channels] = hid[
                pl.ds(c, size * mid * ROW), :
            ].astype(jnp.bfloat16)
        shifted = taps[...].reshape(size, mid, ROW, 3 * channels)
        second = b2_ref[...]
        for a in range(3):
            rows = shifted[:, a:a + last].reshape(size * last * ROW, 3 * channels)
            second = second + jnp.dot(rows, w2_ref[a], preferred_element_type=jnp.float32)
        second = second.reshape(size, last, ROW, -1)[:, :, :last, :]
        out_ref[here] = second.reshape(size, last * last, -1).astype(jnp.bfloat16)

    for copy in list(near_copies.values()) + list(far_copies.values()):
        copy.wait_send()


def encode(part, w1, b1, w2, b2, chips):
    cells = part.shape[1]
    channels = w2.shape[-1]
    hidden = w1.shape[-1]
    size = BLK_DEV // CHUNKS
    rows = size * (PAD_SIDE - 2) * ROW
    packed = -(-(size + 1) * (cells // 2) // ROW) * ROW
    semaphores = [pltpu.SemaphoreType.DMA((CHUNKS, chips))] * 4
    return pl.pallas_call(
        functools.partial(encode_kernel, chips),
        out_shape=jax.ShapeDtypeStruct((BLK_DEV, SIDE * SIDE, channels), jnp.bfloat16),
        in_specs=[VMEM] * 5,
        out_specs=VMEM,
        scratch_shapes=[
            pltpu.VMEM((chips, BLK_DEV, cells, LANES), jnp.bfloat16),
            pltpu.VMEM((BLK_DEV, cells, LANES), jnp.float32),
            pltpu.VMEM((chips - 1, CHUNKS, packed, LANES), jnp.bfloat16),
            pltpu.VMEM((chips - 1, CHUNKS, packed, LANES), jnp.bfloat16),
            pltpu.VMEM((cells + ROW, LANES), jnp.float32),
            pltpu.VMEM((size, PAD_SIDE, ROW, 3 * LANES), jnp.bfloat16),
            pltpu.VMEM((rows + ROW, hidden), jnp.float32),
            pltpu.VMEM((rows, 3 * hidden), jnp.bfloat16),
        ] + semaphores,
        compiler_params=pltpu.CompilerParams(
            collective_id=1, has_side_effects=True, vmem_limit_bytes=40 << 20
        ),
        name="reduce_and_encode",
    )(part, w1, b1, w2, b2)


def strips(
    frames,
    regrid_mats,
    pair_source,
    pair_matrix,
    pair_device,
    pair_local,
    w_first,
    b_first,
    w_second,
    b_second,
):
    devices = lax.axis_size("space")
    strip_blocks = frames.shape[3] // SB
    row_blocks = strip_blocks * devices
    table = jnp.stack([pair_source, pair_matrix, pair_device[:, 0], pair_local])
    tables, mats, sources = gather_tables(table, regrid_mats, frames[0], devices, strip_blocks)
    part = regrid(tables, sources, mats, devices * BLK_DEV, strip_blocks, row_blocks)
    lift = LANES - w_first.shape[2]
    w1 = jnp.pad(w_first, ((0, 0), (0, 0), (0, lift), (0, 0))).reshape(3, 3 * LANES, -1)
    w2 = w_second.reshape(3, -1, w_second.shape[-1])
    out = encode(part, w1, b_first[None], w2, b_second[None], devices // 2)
    return out[None]


def conv_valid(inputs, weights, layout):
    return lax.conv_general_dilated(
        inputs,
        weights,
        (1, 1),
        "VALID",
        dimension_numbers=layout,
        preferred_element_type=jnp.float32,
    )


def per_device(
    frames,
    regrid_mats,
    pair_source,
    pair_matrix,
    pair_device,
    pair_local,
    w_first,
    b_first,
    w_second,
    b_second,
):
    devices = lax.axis_size("space")
    band_rows = lax.all_to_all(frames, "space", split_axis=2, concat_axis=3, tiled=True)
    local_times = band_rows.shape[0]
    variables = band_rows.shape[1]
    source = band_rows.reshape(local_times, variables, -1, SB)
    pair_count = pair_source.shape[0]
    capacity = max(2, 3 * pair_count // (2 * devices))
    flat_count = devices * capacity
    target = pair_device[:, 0]
    matches = (target[:, None] == jnp.arange(devices, dtype=jnp.int32)[None, :]).astype(jnp.int32)
    ranking = jnp.sum(matches * (jnp.cumsum(matches, axis=0) - 1), axis=1)
    places = target * capacity + ranking
    block_slots = (
        jnp.full((flat_count,), BLK_DEV, jnp.int32)
        .at[places]
        .set(pair_local)
        .reshape(devices, capacity)
    )
    picked = jnp.take(source, pair_source, axis=2)
    shipped = jnp.transpose(picked, (2, 0, 1, 3))
    outgoing = (
        jnp.zeros((flat_count, local_times, variables, SB), jnp.bfloat16).at[places].set(shipped)
    )
    outgoing = outgoing.reshape(devices, capacity, local_times, variables, SB)
    matrix_slots = (
        jnp.zeros((flat_count,), jnp.int32).at[places].set(pair_matrix).reshape(devices, capacity)
    )
    rows_part = lax.all_to_all(outgoing, "space", split_axis=0, concat_axis=0, tiled=True)
    matrix_part = lax.all_to_all(matrix_slots, "space", split_axis=0, concat_axis=0, tiled=True)
    block_part = lax.all_to_all(block_slots, "space", split_axis=0, concat_axis=0, tiled=True)
    matrices = jnp.take(regrid_mats, matrix_part, axis=0)
    partial_value = jnp.einsum(
        "nktvs,nksc->nktvc", rows_part, matrices, preferred_element_type=jnp.float32
    ).astype(jnp.bfloat16)
    selector = (
        block_part.reshape(1, flat_count) == jnp.arange(BLK_DEV, dtype=jnp.int32)[:, None]
    ).astype(jnp.bfloat16)
    summed = jnp.dot(
        selector, partial_value.reshape(flat_count, -1), preferred_element_type=jnp.float32
    )
    padded_field = summed.astype(jnp.bfloat16).reshape(
        BLK_DEV * local_times, variables, PAD_SIDE, PAD_SIDE
    )
    first_out = conv_valid(padded_field, w_first, ("NCHW", "HWIO", "NHWC")) + b_first
    hidden = jax.nn.gelu(first_out, approximate=True).astype(jnp.bfloat16)
    second = conv_valid(hidden, w_second, ("NHWC", "HWIO", "NHWC")) + b_second
    result = second.astype(jnp.bfloat16).reshape(BLK_DEV, local_times, SIDE * SIDE, -1)
    return jnp.transpose(result, (1, 0, 2, 3))


def solution(mesh):
    in_specs = (
        P("tm", None, None, "space"),
        P(),
        P("space"),
        P("space"),
        P("space", None),
        P("space"),
        P(),
        P(),
        P(),
        P(),
    )
    out_specs = P("tm", "space", None, None)
    devices = mesh.shape["space"]

    def program(frames, *rest):
        local = (frames.shape[0] // mesh.shape["tm"], frames.shape[3] // devices)
        whole_blocks = local == (1, LANES) and LANES % SB == 0 and devices % 2 == 0
        fits = frames.shape[2] <= 64 and FRONT < frames.shape[1] <= FRONT + TAIL
        body = strips if whole_blocks and fits else per_device
        return jax.shard_map(
            body, mesh=mesh, in_specs=in_specs, out_specs=out_specs, check_vma=False
        )(frames, *rest)

    return program
```

```python
import functools

import jax
import jax.numpy as jnp
from jax import lax
from jax.experimental import pallas as pl
from jax.experimental.pallas import tpu as pltpu
from jax.sharding import PartitionSpec as P

SIDE = 8
SB = 64
BLK_DEV = 12
PAD_SIDE = 12

MESH = pl.DeviceIdType.MESH
VMEM = pl.BlockSpec(memory_space=pltpu.VMEM)
HBM = pl.BlockSpec(memory_space=pltpu.HBM)
LANES = 128
ROW = 16
GROUP = 8
CHUNKS = 3
MATCH = 1 << 20
FRONT = 64
TAIL = 16


def greet(peers):
    barrier = pltpu.get_barrier_semaphore()
    for peer in peers:
        pl.semaphore_signal(barrier, inc=1, device_id={"space": peer}, device_id_type=MESH)
    pl.semaphore_wait(barrier, len(peers))


def table_kernel(
    devices, table_ref, mats_hbm, frames_hbm, all_ref, turned_ref, cells_ref,
    mats_ref, frames_ref, wide, load_sem, send_sem, recv_sem,
):
    me = lax.axis_index("space")
    loads = [
        pltpu.make_async_copy(mats_hbm, mats_ref, load_sem.at[0]),
        pltpu.make_async_copy(frames_hbm, frames_ref, load_sem.at[1]),
    ]
    for load in loads:
        load.start()
    barrier = pltpu.get_barrier_semaphore()
    for step in range(1, devices):
        peer = lax.rem(me + step, devices)
        pl.semaphore_signal(barrier, inc=1, device_id={"space": peer}, device_id_type=MESH)
    variables, lats, lanes = frames_ref.shape
    padded = cells_ref.shape[1]
    wide[pl.ds(variables * lats, (padded - variables) * lats), :] = jnp.zeros(
        ((padded - variables) * lats, lanes), jnp.float32
    )
    loads[0].wait()
    strip_blocks = turned_ref.shape[0] // mats_ref.shape[0]

    @pl.loop(0, mats_ref.shape[0])
    def _(m):
        matrix = mats_ref[m].astype(jnp.float32)
        blank = jnp.zeros_like(matrix)
        for place in range(strip_blocks):
            stack = [matrix if other == place else blank for other in range(strip_blocks)]
            turned_ref[m * strip_blocks + place] = (
                jnp.concatenate(stack, axis=0).T.astype(jnp.bfloat16)
            )

    loads[1].wait()

    @pl.loop(0, variables)
    def _(v):
        wide[pl.ds(pl.multiple_of(v * lats, lats), lats), :] = frames_ref[v].astype(jnp.float32)

    pl.semaphore_wait(barrier, devices - 1)
    copies = []
    for step in range(1, devices):
        copy = pltpu.make_async_remote_copy(
            src_ref=table_ref,
            dst_ref=all_ref.at[me],
            send_sem=send_sem.at[step],
            recv_sem=recv_sem.at[step],
            device_id={"space": lax.rem(me + step, devices)},
            device_id_type=MESH,
        )
        copy.start()
        copies.append(copy)
    all_ref[me] = table_ref[...]

    @pl.loop(0, lats, unroll=4)
    def _(lat):
        cells_ref[lat] = wide[pl.ds(lat, padded, stride=lats), :].astype(jnp.bfloat16)

    for copy in copies:
        copy.wait()


def gather_tables(table, mats, frames, devices, strip_blocks):
    variables, lats, lanes = frames.shape
    padded = -(-variables // 16) * 16
    turned = (mats.shape[0] * strip_blocks, mats.shape[2], strip_blocks * mats.shape[1])
    return pl.pallas_call(
        functools.partial(table_kernel, devices),
        out_shape=(
            jax.ShapeDtypeStruct((devices,) + table.shape, table.dtype),
            jax.ShapeDtypeStruct(turned, mats.dtype),
            jax.ShapeDtypeStruct((lats, padded, lanes), frames.dtype),
        ),
        in_specs=[VMEM, HBM, HBM],
        out_specs=(VMEM, VMEM, VMEM),
        scratch_shapes=[
            pltpu.VMEM(mats.shape, mats.dtype),
            pltpu.VMEM(frames.shape, frames.dtype),
            pltpu.VMEM((padded * lats, lanes), jnp.float32),
            pltpu.SemaphoreType.DMA((2,)),
            pltpu.SemaphoreType.DMA((devices,)),
            pltpu.SemaphoreType.DMA((devices,)),
        ],
        compiler_params=pltpu.CompilerParams(collective_id=0, has_side_effects=True, vmem_limit_bytes=24 << 20),
        name="pair_tables",
    )(table, mats, frames)


def regrid_kernel(
    strip_blocks, row_blocks, table_ref, cells_ref, mats_ref, out_ref,
    total, words_v, words_s, chosen, sem,
):
    devices, _, pairs = table_ref.shape
    lats, padded, _ = cells_ref.shape
    blocks = out_ref.shape[0]
    me = lax.axis_index("space")
    source = table_ref[:, 0, :]
    matrix = table_ref[:, 1, :]
    target = table_ref[:, 2, :] * BLK_DEV + table_ref[:, 3, :]
    band = lax.broadcasted_iota(jnp.int32, (devices, pairs), 0)
    lat = band * (lats // devices) + source // row_blocks
    place = source % row_blocks
    mine = (place // strip_blocks) == me
    word = target * 2048 + lat * 32 + matrix * strip_blocks + place % strip_blocks
    words_v[...] = word + jnp.where(mine, MATCH, 0)
    move = pltpu.make_async_copy(words_v, words_s, sem)
    move.start()
    move.wait()

    def scan_row(row, count):
        def scan(step, count):
            clear = total.shape[0] // (devices * (pairs // 16))
            first = (row * (pairs // 16) + step) * clear
            for b in range(clear):
                total[first + b] = jnp.zeros(total.shape[1:], jnp.float32)
            values = [words_s[row, step * 16 + lane] for lane in range(16)]
            places = [count]
            for value in values:
                places.append(places[-1] + (value >> 20))
            for value, place in zip(values, places):
                chosen[place] = value
            return places[-1]

        return lax.fori_loop(0, pairs // 16, scan, count)

    count = lax.fori_loop(0, devices, scan_row, 0)
    for extra in range(GROUP):
        chosen[count + extra] = blocks * 2048

    @pl.loop(0, (count + GROUP - 1) // GROUP)
    def _(step):
        products, homes = [], []
        for lane in range(GROUP):
            value = chosen[step * GROUP + lane] & (MATCH - 1)
            homes.append(value >> 11)
            products.append(
                lax.dot_general(
                    mats_ref[value & 31], cells_ref[(value >> 5) & 63], (((1,), (1,)), ((), ())),
                    preferred_element_type=jnp.float32,
                )
            )
        for home, product in zip(homes, products):
            total[home, :, :padded] += product

    @pl.loop(0, blocks, unroll=4)
    def _(b):
        out_ref[b] = total[b].astype(jnp.bfloat16)


def regrid(tables, sources, mats, blocks, strip_blocks, row_blocks):
    devices, _, pairs = tables.shape
    cells = mats.shape[1]
    steps = devices * (pairs // 16)
    held = -(-(blocks + 1) // steps) * steps
    return pl.pallas_call(
        functools.partial(regrid_kernel, strip_blocks, row_blocks),
        out_shape=jax.ShapeDtypeStruct((blocks, cells, LANES), jnp.bfloat16),
        in_specs=[VMEM] * 3,
        out_specs=VMEM,
        scratch_shapes=[
            pltpu.VMEM((held, cells, LANES), jnp.float32),
            pltpu.VMEM((devices, pairs), jnp.int32),
            pltpu.SMEM((devices, pairs), jnp.int32),
            pltpu.SMEM((devices * pairs + GROUP,), jnp.int32),
            pltpu.SemaphoreType.DMA,
        ],
        compiler_params=pltpu.CompilerParams(vmem_limit_bytes=40 << 20),
        name="regrid_pairs",
    )(tables, sources, mats)


def pack_fields(fields):
    half = fields[0].shape[0] // 2
    lane = lax.broadcasted_iota(jnp.int32, (half, LANES), 1)
    rest = jnp.zeros((half, LANES), jnp.float32)
    rows = []
    for b, field in enumerate(fields):
        upper, lower = field[:half], field[half:]
        rows.append(jnp.where(lane < FRONT, upper, pltpu.roll(lower, FRONT, 1)))
        for side, piece in enumerate((upper, lower)):
            start = (2 * b + side) * TAIL
            moved = pltpu.roll(piece, (start - FRONT) % LANES, 1)
            rest = jnp.where((lane >= start) & (lane < start + TAIL), moved, rest)
    rows.append(rest)
    spare = -len(rows) * half % ROW
    if spare:
        rows.append(jnp.zeros((spare, LANES), jnp.float32))
    return jnp.concatenate(rows, axis=0)


def unpack_field(packed, b, size, cells):
    half = cells // 2
    lane = lax.broadcasted_iota(jnp.int32, (half, LANES), 1)
    front = packed[b * half:(b + 1) * half]
    rest = packed[size * half:(size + 1) * half]
    pieces = []
    for side in range(2):
        start = (2 * b + side) * TAIL
        head = pltpu.roll(front, FRONT, 1) if side else front
        tail = pltpu.roll(rest, (FRONT - start) % LANES, 1)
        tail = jnp.where(lane < FRONT + TAIL, tail, 0.0)
        pieces.append(jnp.where(lane < FRONT, head, tail))
    return jnp.concatenate(pieces, axis=0)


def encode_kernel(
    chips, part_ref, w1_ref, b1_ref, w2_ref, b2_ref, out_ref,
    near, own, sums, far, flat, wide, hid, taps,
    near_send, near_recv, far_send, far_recv,
):
    me = lax.axis_index("space")
    chip, core = me // 2, lax.rem(me, 2)
    size = BLK_DEV // CHUNKS
    cells = part_ref.shape[1]
    order = list(range(1, chips)) + [0]
    peers = [lax.rem(chip + step, chips) for step in range(chips)]
    sibling = chip * 2 + 1 - core
    greet([sibling] + [peers[step] * 2 + core for step in range(1, chips)])

    near_copies = {}
    for chunk in range(CHUNKS):
        for step in order:
            first = (peers[step] * 2 + 1 - core) * BLK_DEV + chunk * size
            copy = pltpu.make_async_remote_copy(
                src_ref=part_ref.at[pl.ds(first, size)],
                dst_ref=near.at[step, pl.ds(chunk * size, size)],
                send_sem=near_send.at[chunk, step],
                recv_sem=near_recv.at[chunk, step],
                device_id={"space": sibling},
                device_id_type=MESH,
            )
            copy.start()
            near_copies[chunk, step] = copy

    far_copies = {}
    for chunk in range(CHUNKS):
        for step in order:
            near_copies[chunk, step].wait_recv()
            first = (peers[step] * 2 + core) * BLK_DEV + chunk * size
            here = pl.ds(chunk * size, size)
            fields = [
                part_ref[first + b].astype(jnp.float32)
                + near[step, chunk * size + b].astype(jnp.float32)
                for b in range(size)
            ]
            if step == 0:
                for b in range(size):
                    own[chunk * size + b] = fields[b]
            else:
                sums[step - 1, chunk] = pack_fields(fields).astype(jnp.bfloat16)
                copy = pltpu.make_async_remote_copy(
                    src_ref=sums.at[step - 1, chunk],
                    dst_ref=far.at[step - 1, chunk],
                    send_sem=far_send.at[chunk, step],
                    recv_sem=far_recv.at[chunk, step],
                    device_id={"space": peers[step] * 2 + core},
                    device_id_type=MESH,
                )
                copy.start()
                far_copies[chunk, step] = copy

    side = PAD_SIDE
    mid = side - 2
    last = side - 4
    for chunk in range(CHUNKS):
        here = pl.ds(chunk * size, size)
        for step in range(1, chips):
            far_copies[chunk, step].wait_recv()
        packed = far[0, chunk].astype(jnp.float32)
        for step in range(1, chips - 1):
            packed = packed + far[step, chunk].astype(jnp.float32)
        for b in range(size):
            flat[pl.ds(0, cells), :] = own[chunk * size + b] + unpack_field(packed, b, size, cells)
            for i in range(side):
                for c in range(3):
                    wide[b, i, :, c * LANES:(c + 1) * LANES] = flat[
                        pl.ds(i * side + c, ROW), :
                    ].astype(jnp.bfloat16)
        first_out = b1_ref[...]
        for a in range(3):
            rows = wide[:, a:a + mid].reshape(size * mid * ROW, 3 * LANES)
            first_out = first_out + jnp.dot(rows, w1_ref[a], preferred_element_type=jnp.float32)
        hid[pl.ds(0, size * mid * ROW), :] = jax.nn.gelu(first_out, approximate=True)
        channels = hid.shape[1]
        for c in range(3):
            taps[:, c * channels:(c + 1) * channels] = hid[
                pl.ds(c, size * mid * ROW), :
            ].astype(jnp.bfloat16)
        shifted = taps[...].reshape(size, mid, ROW, 3 * channels)
        second = b2_ref[...]
        for a in range(3):
            rows = shifted[:, a:a + last].reshape(size * last * ROW, 3 * channels)
            second = second + jnp.dot(rows, w2_ref[a], preferred_element_type=jnp.float32)
        second = second.reshape(size, last, ROW, -1)[:, :, :last, :]
        out_ref[here] = second.reshape(size, last * last, -1).astype(jnp.bfloat16)

    for copy in list(near_copies.values()) + list(far_copies.values()):
        copy.wait_send()


def encode(part, w1, b1, w2, b2, chips):
    cells = part.shape[1]
    channels = w2.shape[-1]
    hidden = w1.shape[-1]
    size = BLK_DEV // CHUNKS
    rows = size * (PAD_SIDE - 2) * ROW
    packed = -(-(size + 1) * (cells // 2) // ROW) * ROW
    semaphores = [pltpu.SemaphoreType.DMA((CHUNKS, chips))] * 4
    return pl.pallas_call(
        functools.partial(encode_kernel, chips),
        out_shape=jax.ShapeDtypeStruct((BLK_DEV, SIDE * SIDE, channels), jnp.bfloat16),
        in_specs=[VMEM] * 5,
        out_specs=VMEM,
        scratch_shapes=[
            pltpu.VMEM((chips, BLK_DEV, cells, LANES), jnp.bfloat16),
            pltpu.VMEM((BLK_DEV, cells, LANES), jnp.float32),
            pltpu.VMEM((chips - 1, CHUNKS, packed, LANES), jnp.bfloat16),
            pltpu.VMEM((chips - 1, CHUNKS, packed, LANES), jnp.bfloat16),
            pltpu.VMEM((cells + ROW, LANES), jnp.float32),
            pltpu.VMEM((size, PAD_SIDE, ROW, 3 * LANES), jnp.bfloat16),
            pltpu.VMEM((rows + ROW, hidden), jnp.float32),
            pltpu.VMEM((rows, 3 * hidden), jnp.bfloat16),
        ] + semaphores,
        compiler_params=pltpu.CompilerParams(
            collective_id=1, has_side_effects=True, vmem_limit_bytes=40 << 20
        ),
        name="reduce_and_encode",
    )(part, w1, b1, w2, b2)


def strips(
    frames,
    regrid_mats,
    pair_source,
    pair_matrix,
    pair_device,
    pair_local,
    w_first,
    b_first,
    w_second,
    b_second,
):
    devices = lax.axis_size("space")
    strip_blocks = frames.shape[3] // SB
    row_blocks = strip_blocks * devices
    table = jnp.stack([pair_source, pair_matrix, pair_device[:, 0], pair_local])
    tables, mats, sources = gather_tables(table, regrid_mats, frames[0], devices, strip_blocks)
    part = regrid(tables, sources, mats, devices * BLK_DEV, strip_blocks, row_blocks)
    lift = LANES - w_first.shape[2]
    w1 = jnp.pad(w_first, ((0, 0), (0, 0), (0, lift), (0, 0))).reshape(3, 3 * LANES, -1)
    w2 = w_second.reshape(3, -1, w_second.shape[-1])
    out = encode(part, w1, b_first[None], w2, b_second[None], devices // 2)
    return out[None]


def conv_valid(inputs, weights, layout):
    return lax.conv_general_dilated(
        inputs,
        weights,
        (1, 1),
        "VALID",
        dimension_numbers=layout,
        preferred_element_type=jnp.float32,
    )


def per_device(
    frames,
    regrid_mats,
    pair_source,
    pair_matrix,
    pair_device,
    pair_local,
    w_first,
    b_first,
    w_second,
    b_second,
):
    devices = lax.axis_size("space")
    band_rows = lax.all_to_all(frames, "space", split_axis=2, concat_axis=3, tiled=True)
    local_times = band_rows.shape[0]
    variables = band_rows.shape[1]
    source = band_rows.reshape(local_times, variables, -1, SB)
    pair_count = pair_source.shape[0]
    capacity = max(2, 3 * pair_count // (2 * devices))
    flat_count = devices * capacity
    target = pair_device[:, 0]
    matches = (target[:, None] == jnp.arange(devices, dtype=jnp.int32)[None, :]).astype(jnp.int32)
    ranking = jnp.sum(matches * (jnp.cumsum(matches, axis=0) - 1), axis=1)
    places = target * capacity + ranking
    block_slots = (
        jnp.full((flat_count,), BLK_DEV, jnp.int32)
        .at[places]
        .set(pair_local)
        .reshape(devices, capacity)
    )
    picked = jnp.take(source, pair_source, axis=2)
    shipped = jnp.transpose(picked, (2, 0, 1, 3))
    outgoing = (
        jnp.zeros((flat_count, local_times, variables, SB), jnp.bfloat16).at[places].set(shipped)
    )
    outgoing = outgoing.reshape(devices, capacity, local_times, variables, SB)
    matrix_slots = (
        jnp.zeros((flat_count,), jnp.int32).at[places].set(pair_matrix).reshape(devices, capacity)
    )
    rows_part = lax.all_to_all(outgoing, "space", split_axis=0, concat_axis=0, tiled=True)
    matrix_part = lax.all_to_all(matrix_slots, "space", split_axis=0, concat_axis=0, tiled=True)
    block_part = lax.all_to_all(block_slots, "space", split_axis=0, concat_axis=0, tiled=True)
    matrices = jnp.take(regrid_mats, matrix_part, axis=0)
    partial_value = jnp.einsum(
        "nktvs,nksc->nktvc", rows_part, matrices, preferred_element_type=jnp.float32
    ).astype(jnp.bfloat16)
    selector = (
        block_part.reshape(1, flat_count) == jnp.arange(BLK_DEV, dtype=jnp.int32)[:, None]
    ).astype(jnp.bfloat16)
    summed = jnp.dot(
        selector, partial_value.reshape(flat_count, -1), preferred_element_type=jnp.float32
    )
    padded_field = summed.astype(jnp.bfloat16).reshape(
        BLK_DEV * local_times, variables, PAD_SIDE, PAD_SIDE
    )
    first_out = conv_valid(padded_field, w_first, ("NCHW", "HWIO", "NHWC")) + b_first
    hidden = jax.nn.gelu(first_out, approximate=True).astype(jnp.bfloat16)
    second = conv_valid(hidden, w_second, ("NHWC", "HWIO", "NHWC")) + b_second
    result = second.astype(jnp.bfloat16).reshape(BLK_DEV, local_times, SIDE * SIDE, -1)
    return jnp.transpose(result, (1, 0, 2, 3))


def solution(mesh):
    in_specs = (
        P("tm", None, None, "space"),
        P(),
        P("space"),
        P("space"),
        P("space", None),
        P("space"),
        P(),
        P(),
        P(),
        P(),
    )
    out_specs = P("tm", "space", None, None)
    devices = mesh.shape["space"]

    def program(frames, *rest):
        local = (frames.shape[0] // mesh.shape["tm"], frames.shape[3] // devices)
        whole_blocks = local == (1, LANES) and LANES % SB == 0 and devices % 2 == 0
        fits = frames.shape[2] <= 64 and FRONT < frames.shape[1] <= FRONT + TAIL
        body = strips if whole_blocks and fits else per_device
        return jax.shard_map(
            body, mesh=mesh, in_specs=in_specs, out_specs=out_specs, check_vma=False
        )(frames, *rest)

    return program
```

```python
import functools

import jax
import jax.numpy as jnp
from jax import lax
from jax.experimental import pallas as pl
from jax.experimental.pallas import tpu as pltpu
from jax.sharding import PartitionSpec as P

SIDE = 8
SB = 64
BLK_DEV = 12
PAD_SIDE = 12

MESH = pl.DeviceIdType.MESH
VMEM = pl.BlockSpec(memory_space=pltpu.VMEM)
HBM = pl.BlockSpec(memory_space=pltpu.HBM)
LANES = 128
ROW = 16
GROUP = 16
CHUNKS = 3
MATCH = 1 << 20
FRONT = 64
TAIL = 16


def greet(peers):
    barrier = pltpu.get_barrier_semaphore()
    for peer in peers:
        pl.semaphore_signal(barrier, inc=1, device_id={"space": peer}, device_id_type=MESH)
    pl.semaphore_wait(barrier, len(peers))


def table_kernel(
    devices, table_ref, mats_hbm, frames_hbm, all_ref, turned_ref, cells_ref,
    mats_ref, frames_ref, wide, load_sem, send_sem, recv_sem,
):
    me = lax.axis_index("space")
    loads = [
        pltpu.make_async_copy(mats_hbm, mats_ref, load_sem.at[0]),
        pltpu.make_async_copy(frames_hbm, frames_ref, load_sem.at[1]),
    ]
    for load in loads:
        load.start()
    barrier = pltpu.get_barrier_semaphore()
    for step in range(1, devices):
        peer = lax.rem(me + step, devices)
        pl.semaphore_signal(barrier, inc=1, device_id={"space": peer}, device_id_type=MESH)
    variables, lats, lanes = frames_ref.shape
    padded = cells_ref.shape[1]
    wide[pl.ds(variables * lats, (padded - variables) * lats), :] = jnp.zeros(
        ((padded - variables) * lats, lanes), jnp.float32
    )
    loads[0].wait()
    strip_blocks = turned_ref.shape[0] // mats_ref.shape[0]

    @pl.loop(0, mats_ref.shape[0])
    def _(m):
        matrix = mats_ref[m].astype(jnp.float32)
        blank = jnp.zeros_like(matrix)
        for place in range(strip_blocks):
            stack = [matrix if other == place else blank for other in range(strip_blocks)]
            turned_ref[m * strip_blocks + place] = (
                jnp.concatenate(stack, axis=0).T.astype(jnp.bfloat16)
            )

    loads[1].wait()

    @pl.loop(0, variables)
    def _(v):
        wide[pl.ds(pl.multiple_of(v * lats, lats), lats), :] = frames_ref[v].astype(jnp.float32)

    pl.semaphore_wait(barrier, devices - 1)
    copies = []
    for step in range(1, devices):
        copy = pltpu.make_async_remote_copy(
            src_ref=table_ref,
            dst_ref=all_ref.at[me],
            send_sem=send_sem.at[step],
            recv_sem=recv_sem.at[step],
            device_id={"space": lax.rem(me + step, devices)},
            device_id_type=MESH,
        )
        copy.start()
        copies.append(copy)
    all_ref[me] = table_ref[...]

    @pl.loop(0, lats, unroll=4)
    def _(lat):
        cells_ref[lat] = wide[pl.ds(lat, padded, stride=lats), :].astype(jnp.bfloat16)

    for copy in copies:
        copy.wait()


def gather_tables(table, mats, frames, devices, strip_blocks):
    variables, lats, lanes = frames.shape
    padded = -(-variables // 16) * 16
    turned = (mats.shape[0] * strip_blocks, mats.shape[2], strip_blocks * mats.shape[1])
    return pl.pallas_call(
        functools.partial(table_kernel, devices),
        out_shape=(
            jax.ShapeDtypeStruct((devices,) + table.shape, table.dtype),
            jax.ShapeDtypeStruct(turned, mats.dtype),
            jax.ShapeDtypeStruct((lats, padded, lanes), frames.dtype),
        ),
        in_specs=[VMEM, HBM, HBM],
        out_specs=(VMEM, VMEM, VMEM),
        scratch_shapes=[
            pltpu.VMEM(mats.shape, mats.dtype),
            pltpu.VMEM(frames.shape, frames.dtype),
            pltpu.VMEM((padded * lats, lanes), jnp.float32),
            pltpu.SemaphoreType.DMA((2,)),
            pltpu.SemaphoreType.DMA((devices,)),
            pltpu.SemaphoreType.DMA((devices,)),
        ],
        compiler_params=pltpu.CompilerParams(collective_id=0, has_side_effects=True, vmem_limit_bytes=24 << 20),
        name="pair_tables",
    )(table, mats, frames)


def regrid_kernel(
    strip_blocks, row_blocks, table_ref, cells_ref, mats_ref, out_ref,
    total, words_v, words_s, chosen, sem,
):
    devices, _, pairs = table_ref.shape
    lats, padded, _ = cells_ref.shape
    blocks = out_ref.shape[0]
    me = lax.axis_index("space")
    source = table_ref[:, 0, :]
    matrix = table_ref[:, 1, :]
    target = table_ref[:, 2, :] * BLK_DEV + table_ref[:, 3, :]
    band = lax.broadcasted_iota(jnp.int32, (devices, pairs), 0)
    lat = band * (lats // devices) + source // row_blocks
    place = source % row_blocks
    mine = (place // strip_blocks) == me
    word = target * 2048 + lat * 32 + matrix * strip_blocks + place % strip_blocks
    words_v[...] = word + jnp.where(mine, MATCH, 0)
    move = pltpu.make_async_copy(words_v, words_s, sem)
    move.start()
    move.wait()

    def scan_row(row, count):
        def scan(step, count):
            clear = total.shape[0] // (devices * (pairs // 16))
            first = (row * (pairs // 16) + step) * clear
            for b in range(clear):
                total[first + b] = jnp.zeros(total.shape[1:], jnp.float32)
            values = [words_s[row, step * 16 + lane] for lane in range(16)]
            places = [count]
            for value in values:
                places.append(places[-1] + (value >> 20))
            for value, place in zip(values, places):
                chosen[place] = value
            return places[-1]

        return lax.fori_loop(0, pairs // 16, scan, count)

    count = lax.fori_loop(0, devices, scan_row, 0)
    for extra in range(GROUP):
        chosen[count + extra] = blocks * 2048

    @pl.loop(0, (count + GROUP - 1) // GROUP)
    def _(step):
        products, homes = [], []
        for lane in range(GROUP):
            value = chosen[step * GROUP + lane] & (MATCH - 1)
            homes.append(value >> 11)
            products.append(
                lax.dot_general(
                    mats_ref[value & 31], cells_ref[(value >> 5) & 63], (((1,), (1,)), ((), ())),
                    preferred_element_type=jnp.float32,
                )
            )
        for home, product in zip(homes, products):
            total[home, :, :padded] += product

    @pl.loop(0, blocks, unroll=4)
    def _(b):
        out_ref[b] = total[b].astype(jnp.bfloat16)


def regrid(tables, sources, mats, blocks, strip_blocks, row_blocks):
    devices, _, pairs = tables.shape
    cells = mats.shape[1]
    steps = devices * (pairs // 16)
    held = -(-(blocks + 1) // steps) * steps
    return pl.pallas_call(
        functools.partial(regrid_kernel, strip_blocks, row_blocks),
        out_shape=jax.ShapeDtypeStruct((blocks, cells, LANES), jnp.bfloat16),
        in_specs=[VMEM] * 3,
        out_specs=VMEM,
        scratch_shapes=[
            pltpu.VMEM((held, cells, LANES), jnp.float32),
            pltpu.VMEM((devices, pairs), jnp.int32),
            pltpu.SMEM((devices, pairs), jnp.int32),
            pltpu.SMEM((devices * pairs + GROUP,), jnp.int32),
            pltpu.SemaphoreType.DMA,
        ],
        compiler_params=pltpu.CompilerParams(vmem_limit_bytes=40 << 20),
        name="regrid_pairs",
    )(tables, sources, mats)


def pack_fields(fields):
    half = fields[0].shape[0] // 2
    lane = lax.broadcasted_iota(jnp.int32, (half, LANES), 1)
    rest = jnp.zeros((half, LANES), jnp.float32)
    rows = []
    for b, field in enumerate(fields):
        upper, lower = field[:half], field[half:]
        rows.append(jnp.where(lane < FRONT, upper, pltpu.roll(lower, FRONT, 1)))
        for side, piece in enumerate((upper, lower)):
            start = (2 * b + side) * TAIL
            moved = pltpu.roll(piece, (start - FRONT) % LANES, 1)
            rest = jnp.where((lane >= start) & (lane < start + TAIL), moved, rest)
    rows.append(rest)
    spare = -len(rows) * half % ROW
    if spare:
        rows.append(jnp.zeros((spare, LANES), jnp.float32))
    return jnp.concatenate(rows, axis=0)


def unpack_field(packed, b, size, cells):
    half = cells // 2
    lane = lax.broadcasted_iota(jnp.int32, (half, LANES), 1)
    front = packed[b * half:(b + 1) * half]
    rest = packed[size * half:(size + 1) * half]
    pieces = []
    for side in range(2):
        start = (2 * b + side) * TAIL
        head = pltpu.roll(front, FRONT, 1) if side else front
        tail = pltpu.roll(rest, (FRONT - start) % LANES, 1)
        tail = jnp.where(lane < FRONT + TAIL, tail, 0.0)
        pieces.append(jnp.where(lane < FRONT, head, tail))
    return jnp.concatenate(pieces, axis=0)


def encode_kernel(
    chips, part_ref, w1_ref, b1_ref, w2_ref, b2_ref, out_ref,
    near, own, sums, far, flat, wide, hid, taps,
    near_send, near_recv, far_send, far_recv,
):
    me = lax.axis_index("space")
    chip, core = me // 2, lax.rem(me, 2)
    size = BLK_DEV // CHUNKS
    cells = part_ref.shape[1]
    order = list(range(1, chips)) + [0]
    peers = [lax.rem(chip + step, chips) for step in range(chips)]
    sibling = chip * 2 + 1 - core
    greet([sibling] + [peers[step] * 2 + core for step in range(1, chips)])

    near_copies = {}
    for chunk in range(CHUNKS):
        for step in order:
            first = (peers[step] * 2 + 1 - core) * BLK_DEV + chunk * size
            copy = pltpu.make_async_remote_copy(
                src_ref=part_ref.at[pl.ds(first, size)],
                dst_ref=near.at[step, pl.ds(chunk * size, size)],
                send_sem=near_send.at[chunk, step],
                recv_sem=near_recv.at[chunk, step],
                device_id={"space": sibling},
                device_id_type=MESH,
            )
            copy.start()
            near_copies[chunk, step] = copy

    far_copies = {}
    for chunk in range(CHUNKS):
        for step in order:
            near_copies[chunk, step].wait_recv()
            first = (peers[step] * 2 + core) * BLK_DEV + chunk * size
            here = pl.ds(chunk * size, size)
            fields = [
                part_ref[first + b].astype(jnp.float32)
                + near[step, chunk * size + b].astype(jnp.float32)
                for b in range(size)
            ]
            if step == 0:
                for b in range(size):
                    own[chunk * size + b] = fields[b]
            else:
                sums[step - 1, chunk] = pack_fields(fields).astype(jnp.bfloat16)
                copy = pltpu.make_async_remote_copy(
                    src_ref=sums.at[step - 1, chunk],
                    dst_ref=far.at[step - 1, chunk],
                    send_sem=far_send.at[chunk, step],
                    recv_sem=far_recv.at[chunk, step],
                    device_id={"space": peers[step] * 2 + core},
                    device_id_type=MESH,
                )
                copy.start()
                far_copies[chunk, step] = copy

    side = PAD_SIDE
    mid = side - 2
    last = side - 4
    for chunk in range(CHUNKS):
        here = pl.ds(chunk * size, size)
        for step in range(1, chips):
            far_copies[chunk, step].wait_recv()
        packed = far[0, chunk].astype(jnp.float32)
        for step in range(1, chips - 1):
            packed = packed + far[step, chunk].astype(jnp.float32)
        for b in range(size):
            flat[pl.ds(0, cells), :] = own[chunk * size + b] + unpack_field(packed, b, size, cells)
            for i in range(side):
                for c in range(3):
                    wide[b, i, :, c * LANES:(c + 1) * LANES] = flat[
                        pl.ds(i * side + c, ROW), :
                    ].astype(jnp.bfloat16)
        first_out = b1_ref[...]
        for a in range(3):
            rows = wide[:, a:a + mid].reshape(size * mid * ROW, 3 * LANES)
            first_out = first_out + jnp.dot(rows, w1_ref[a], preferred_element_type=jnp.float32)
        hid[pl.ds(0, size * mid * ROW), :] = jax.nn.gelu(first_out, approximate=True)
        channels = hid.shape[1]
        for c in range(3):
            taps[:, c * channels:(c + 1) * channels] = hid[
                pl.ds(c, size * mid * ROW), :
            ].astype(jnp.bfloat16)
        shifted = taps[...].reshape(size, mid, ROW, 3 * channels)
        second = b2_ref[...]
        for a in range(3):
            rows = shifted[:, a:a + last].reshape(size * last * ROW, 3 * channels)
            second = second + jnp.dot(rows, w2_ref[a], preferred_element_type=jnp.float32)
        second = second.reshape(size, last, ROW, -1)[:, :, :last, :]
        out_ref[here] = second.reshape(size, last * last, -1).astype(jnp.bfloat16)

    for copy in list(near_copies.values()) + list(far_copies.values()):
        copy.wait_send()


def encode(part, w1, b1, w2, b2, chips):
    cells = part.shape[1]
    channels = w2.shape[-1]
    hidden = w1.shape[-1]
    size = BLK_DEV // CHUNKS
    rows = size * (PAD_SIDE - 2) * ROW
    packed = -(-(size + 1) * (cells // 2) // ROW) * ROW
    semaphores = [pltpu.SemaphoreType.DMA((CHUNKS, chips))] * 4
    return pl.pallas_call(
        functools.partial(encode_kernel, chips),
        out_shape=jax.ShapeDtypeStruct((BLK_DEV, SIDE * SIDE, channels), jnp.bfloat16),
        in_specs=[VMEM] * 5,
        out_specs=VMEM,
        scratch_shapes=[
            pltpu.VMEM((chips, BLK_DEV, cells, LANES), jnp.bfloat16),
            pltpu.VMEM((BLK_DEV, cells, LANES), jnp.float32),
            pltpu.VMEM((chips - 1, CHUNKS, packed, LANES), jnp.bfloat16),
            pltpu.VMEM((chips - 1, CHUNKS, packed, LANES), jnp.bfloat16),
            pltpu.VMEM((cells + ROW, LANES), jnp.float32),
            pltpu.VMEM((size, PAD_SIDE, ROW, 3 * LANES), jnp.bfloat16),
            pltpu.VMEM((rows + ROW, hidden), jnp.float32),
            pltpu.VMEM((rows, 3 * hidden), jnp.bfloat16),
        ] + semaphores,
        compiler_params=pltpu.CompilerParams(
            collective_id=1, has_side_effects=True, vmem_limit_bytes=40 << 20
        ),
        name="reduce_and_encode",
    )(part, w1, b1, w2, b2)


def strips(
    frames,
    regrid_mats,
    pair_source,
    pair_matrix,
    pair_device,
    pair_local,
    w_first,
    b_first,
    w_second,
    b_second,
):
    devices = lax.axis_size("space")
    strip_blocks = frames.shape[3] // SB
    row_blocks = strip_blocks * devices
    table = jnp.stack([pair_source, pair_matrix, pair_device[:, 0], pair_local])
    tables, mats, sources = gather_tables(table, regrid_mats, frames[0], devices, strip_blocks)
    part = regrid(tables, sources, mats, devices * BLK_DEV, strip_blocks, row_blocks)
    lift = LANES - w_first.shape[2]
    w1 = jnp.pad(w_first, ((0, 0), (0, 0), (0, lift), (0, 0))).reshape(3, 3 * LANES, -1)
    w2 = w_second.reshape(3, -1, w_second.shape[-1])
    out = encode(part, w1, b_first[None], w2, b_second[None], devices // 2)
    return out[None]


def conv_valid(inputs, weights, layout):
    return lax.conv_general_dilated(
        inputs,
        weights,
        (1, 1),
        "VALID",
        dimension_numbers=layout,
        preferred_element_type=jnp.float32,
    )


def per_device(
    frames,
    regrid_mats,
    pair_source,
    pair_matrix,
    pair_device,
    pair_local,
    w_first,
    b_first,
    w_second,
    b_second,
):
    devices = lax.axis_size("space")
    band_rows = lax.all_to_all(frames, "space", split_axis=2, concat_axis=3, tiled=True)
    local_times = band_rows.shape[0]
    variables = band_rows.shape[1]
    source = band_rows.reshape(local_times, variables, -1, SB)
    pair_count = pair_source.shape[0]
    capacity = max(2, 3 * pair_count // (2 * devices))
    flat_count = devices * capacity
    target = pair_device[:, 0]
    matches = (target[:, None] == jnp.arange(devices, dtype=jnp.int32)[None, :]).astype(jnp.int32)
    ranking = jnp.sum(matches * (jnp.cumsum(matches, axis=0) - 1), axis=1)
    places = target * capacity + ranking
    block_slots = (
        jnp.full((flat_count,), BLK_DEV, jnp.int32)
        .at[places]
        .set(pair_local)
        .reshape(devices, capacity)
    )
    picked = jnp.take(source, pair_source, axis=2)
    shipped = jnp.transpose(picked, (2, 0, 1, 3))
    outgoing = (
        jnp.zeros((flat_count, local_times, variables, SB), jnp.bfloat16).at[places].set(shipped)
    )
    outgoing = outgoing.reshape(devices, capacity, local_times, variables, SB)
    matrix_slots = (
        jnp.zeros((flat_count,), jnp.int32).at[places].set(pair_matrix).reshape(devices, capacity)
    )
    rows_part = lax.all_to_all(outgoing, "space", split_axis=0, concat_axis=0, tiled=True)
    matrix_part = lax.all_to_all(matrix_slots, "space", split_axis=0, concat_axis=0, tiled=True)
    block_part = lax.all_to_all(block_slots, "space", split_axis=0, concat_axis=0, tiled=True)
    matrices = jnp.take(regrid_mats, matrix_part, axis=0)
    partial_value = jnp.einsum(
        "nktvs,nksc->nktvc", rows_part, matrices, preferred_element_type=jnp.float32
    ).astype(jnp.bfloat16)
    selector = (
        block_part.reshape(1, flat_count) == jnp.arange(BLK_DEV, dtype=jnp.int32)[:, None]
    ).astype(jnp.bfloat16)
    summed = jnp.dot(
        selector, partial_value.reshape(flat_count, -1), preferred_element_type=jnp.float32
    )
    padded_field = summed.astype(jnp.bfloat16).reshape(
        BLK_DEV * local_times, variables, PAD_SIDE, PAD_SIDE
    )
    first_out = conv_valid(padded_field, w_first, ("NCHW", "HWIO", "NHWC")) + b_first
    hidden = jax.nn.gelu(first_out, approximate=True).astype(jnp.bfloat16)
    second = conv_valid(hidden, w_second, ("NHWC", "HWIO", "NHWC")) + b_second
    result = second.astype(jnp.bfloat16).reshape(BLK_DEV, local_times, SIDE * SIDE, -1)
    return jnp.transpose(result, (1, 0, 2, 3))


def solution(mesh):
    in_specs = (
        P("tm", None, None, "space"),
        P(),
        P("space"),
        P("space"),
        P("space", None),
        P("space"),
        P(),
        P(),
        P(),
        P(),
    )
    out_specs = P("tm", "space", None, None)
    devices = mesh.shape["space"]

    def program(frames, *rest):
        local = (frames.shape[0] // mesh.shape["tm"], frames.shape[3] // devices)
        whole_blocks = local == (1, LANES) and LANES % SB == 0 and devices % 2 == 0
        fits = frames.shape[2] <= 64 and FRONT < frames.shape[1] <= FRONT + TAIL
        body = strips if whole_blocks and fits else per_device
        return jax.shard_map(
            body, mesh=mesh, in_specs=in_specs, out_specs=out_specs, check_vma=False
        )(frames, *rest)

    return program
```
